128 devices in a mesh: leaf: 4 (over y), sep: 32 (over x, z, core).
Axes of the slice: x: 4, y: 4, z: 4, core: 2. Of those that a mesh axis runs over, the one named last changes fastest.
Arguments:
- leaf_rhs: float32 [128, 16, 1024], P(('leaf', 'sep')), may hold values from -6 to 6
- leaf_inv: float32 [128, 1024, 1024], P(('leaf', 'sep'))
- update_blocks: float32 [128, 1024, 1024], P(('leaf', 'sep')), may hold values from -0.1875 to 0.1875
- row_map: int32 [128, 1024], P(('leaf', 'sep')), may hold values from 0 to 24575, as said below
- live_rows: int32 [128], P(('leaf', 'sep')), may hold values from 1 to 1024, 81920 in all
- sep_rhs: float32 [16, 6, 4, 32, 32], P(None, None, None, 'sep'), may hold values from -6 to 6
- inv_diag: float32 [6, 4, 32, 32, 4096], P(None, None, 'sep', None, 'leaf')
- panels: float32 [15, 4, 32, 32, 4096], P(None, None, 'sep', None, 'leaf'), may hold values from -0.046875 to 0.046875
Outputs:
- leaf_solution: float32 [128, 16, 1024], P(('leaf', 'sep'))
- sep_solution: float32 [16, 6, 4, 32, 32], P(None, None, None, 'sep')
The draws below stay inside these ranges and needn't reach their ends.
Inputs may be any that keep to these rules, and one draw needn't show every extreme that they name: `row_map`: the 1024 entries of one leaf are distinct global separator rows; writing a row g as k * 4096 + o * 32 + i with 0 <= i < 32, at most 16 entries of one leaf share the same o, and some leaf has exactly 16 with one o.
All inputs are finite; a program needn't handle non-finite values. No bound on the sum of `live_rows` on one device may be relied on, other than what follows from the above.
Results may differ from the reference program's by a relative error of at most 0.0001.
Values sent between devices are 32-bit elements; how exact they have to be, the bound alone decides.
No kernel may reach another device: no remote copies, remote signals or barrier semaphores. Data moves between devices by JAX's collectives and lax.ppermute only.
A program may use at most 128 MiB of HBM per device.

```python
import math
import jax
import jax.numpy as jnp
import numpy as np
from jax import lax

SEP_ORDER = 4096
LEAF_ORDER = 1024
UPD = 1024
VECS = 16
LEVELS = 6
NLEAVES = 128
NPAIRS = 15
SEG = 32
CAP = 16
N_LEAF = 4
N_SEP = 32


def draw_leaf_inv(key, part):
    key = jax.random.fold_in(key, 11)
    array_shape = (NLEAVES, LEAF_ORDER, LEAF_ORDER)
    row_index = lax.broadcasted_iota(jnp.int32, (1, LEAF_ORDER, 1), 1)
    col_index = lax.broadcasted_iota(jnp.int32, (1, 1, LEAF_ORDER), 2)
    noise_part = 0.5 * jax.random.normal(key, array_shape, jnp.float32) / math.sqrt(LEAF_ORDER)
    diag_part = jnp.ones((NLEAVES, LEAF_ORDER, 1), jnp.float32)
    return jnp.where(row_index == col_index, diag_part + noise_part, noise_part)


def draw_inv_diag(key, part):
    key = jax.random.fold_in(key, 13)
    array_shape = (LEVELS, N_LEAF, N_SEP, SEG, SEP_ORDER)
    quarter_index = lax.broadcasted_iota(jnp.int32, (1, N_LEAF, N_SEP, SEG, 1), 1)
    block_index = lax.broadcasted_iota(jnp.int32, (1, N_LEAF, N_SEP, SEG, 1), 2)
    inner_index = lax.broadcasted_iota(jnp.int32, (1, N_LEAF, N_SEP, SEG, 1), 3)
    row_index = (quarter_index * N_SEP + block_index) * SEG + inner_index
    col_index = lax.broadcasted_iota(jnp.int32, (1, 1, 1, 1, SEP_ORDER), 4)
    noise_part = 0.5 * jax.random.normal(key, array_shape, jnp.float32) / math.sqrt(SEP_ORDER)
    diag_part = jnp.ones((LEVELS, N_LEAF, N_SEP, SEG, 1), jnp.float32)
    return jnp.where(row_index == col_index, diag_part + noise_part, noise_part)


def draw_row_map(key, part):
    key = jax.random.fold_in(key, 17)
    owners = NLEAVES
    capacity = CAP
    owner_rows = LEVELS * SEG
    slot_keys = jax.random.split(jax.random.fold_in(key, 1), NLEAVES)
    slot_orders = jax.vmap(lambda one_key: jax.random.permutation(one_key, owners * capacity))(slot_keys)
    first_owner = slot_orders[0] // capacity
    flagged = jnp.where(first_owner == 0, 0, jnp.where(first_owner == owners - 1, 1, 2))
    slot_orders = slot_orders.at[0].set(slot_orders[0][jnp.argsort(flagged, stable=True)])
    chosen = slot_orders[:, :UPD]
    owner_of = chosen // capacity
    within = chosen % capacity
    row_keys = jax.random.split(jax.random.fold_in(key, 2), NLEAVES * owners)
    row_orders = jax.vmap(lambda one_key: jax.random.permutation(one_key, owner_rows))(row_keys)
    row_orders = row_orders.reshape(NLEAVES, owners, owner_rows)
    low_set = row_orders[0, 0]
    row_orders = row_orders.at[0, 0].set(low_set[jnp.argsort(jnp.where(low_set == 0, 0, 1), stable=True)])
    high_set = row_orders[0, owners - 1]
    row_orders = row_orders.at[0, owners - 1].set(high_set[jnp.argsort(jnp.where(high_set == owner_rows - 1, 0, 1), stable=True)])
    leaf_ids = jnp.arange(NLEAVES, dtype=jnp.int32)[:, None]
    picked = row_orders[leaf_ids, owner_of, within]
    level_of = picked // SEG
    inner_of = picked % SEG
    return (level_of * SEP_ORDER + owner_of * SEG + inner_of).astype(jnp.int32)


def block_levels(key, extent, cuts, low, top_value):
    def one(dim, blocks):
        heights = jax.random.uniform(jax.random.fold_in(jax.random.fold_in(key, 6), dim), (blocks,), jnp.float32, low / len(cuts), top_value / len(cuts))
        return jnp.repeat(jnp.exp(heights), extent[dim] // blocks).reshape((-1,) + (1,) * (len(extent) - dim - 1))

    gain = one(*cuts[0])
    for cut in cuts[1:]:
        gain = gain * one(*cut)
    return gain


def length_profile(number_of, total, most, skew):
    weights = [(1 << 20) // math.isqrt(rank ** skew) + 1 for rank in range(2, number_of + 1)]
    spare, holding = total - most - (number_of - 1), [1] * (number_of - 1)
    while spare > 0:
        movable = [i for i in range(number_of - 1) if holding[i] < most]
        pool, budget = sum([weights[i] for i in movable]), spare
        for i in movable:
            addition = min(most - holding[i], max(1, budget * weights[i] // pool), spare)
            holding[i] = holding[i] + addition
            spare = spare - addition
    return np.array([most] + holding)


def ragged_sizes(key, number_of, total, bound, lean):
    if number_of == 2:
        one = jax.random.randint(key, (), max(1, total - bound), min(bound, total - 1) + 1)
        return jnp.stack([one, total - one])
    sizes = jnp.asarray(length_profile(number_of, total, bound, lean), jnp.int32)
    pairs = (number_of - 1) // 2
    donor, receiver = sizes[1:1 + 2 * pairs:2], sizes[2:2 + 2 * pairs:2]
    slack = jnp.minimum(donor - 1, bound - receiver)
    shifted = jax.random.randint(jax.random.fold_in(key, 1), (pairs,), 0, 1 << 20) % (slack + 1)
    sizes = sizes.at[1:1 + 2 * pairs:2].set(donor - shifted).at[2:2 + 2 * pairs:2].set(receiver + shifted)
    return sizes[jax.random.permutation(jax.random.fold_in(key, 2), number_of)]


def gaussian(key, extent, scale, reach, shards=(), kind=jnp.bfloat16):
    entries = scale * jax.random.normal(key, extent, jnp.float32)
    if shards:
        entries = entries * block_levels(key, extent, shards, -0.22, 0.18)
    return jnp.clip(entries, -reach, reach).astype(kind)


def setup_inputs(seed: int = 0) -> dict:
    splits = jax.random.split(jax.random.key(seed), 9)
    return {
        "leaf_rhs": gaussian(splits[0], (NLEAVES, VECS, LEAF_ORDER), 1.0, 6.0, ((0, 128),), jnp.float32),
        "leaf_inv": draw_leaf_inv(jax.random.fold_in(splits[8], 71), 0),
        "update_blocks": gaussian(splits[2], (NLEAVES, LEAF_ORDER, UPD), LEAF_ORDER ** -0.5, 0.1875, ((0, 128),), jnp.float32),
        "row_map": draw_row_map(jax.random.fold_in(splits[8], 71), 0),
        "live_rows": ragged_sizes(splits[4], NLEAVES, NLEAVES * UPD * 5 // 8, UPD, 2).astype(jnp.int32),
        "sep_rhs": gaussian(splits[5], (VECS, LEVELS, N_LEAF, N_SEP, SEG), 1.0, 6.0, ((3, 32),), jnp.float32),
        "inv_diag": draw_inv_diag(jax.random.fold_in(splits[8], 71), 0),
        "panels": gaussian(splits[7], (NPAIRS, N_LEAF, N_SEP, SEG, SEP_ORDER), (4 * SEP_ORDER) ** -0.5, 0.046875, ((2, 32), (4, 4)), jnp.float32),
    }


def pair_start(lower_level, levels):
    return lower_level * (levels - 1) - lower_level * (lower_level - 1) // 2


def pair_index(upper_level, lower_level, levels):
    return pair_start(lower_level, levels) + upper_level - lower_level - 1


def reference(leaf_rhs, leaf_inv, update_blocks, row_map, live_rows, sep_rhs, inv_diag, panels):
    precise = lax.Precision.HIGHEST
    leaf_y = jnp.einsum("nrb,ncb->nrc", leaf_rhs, leaf_inv, precision=precise)
    live_mask = (jnp.arange(UPD, dtype=jnp.int32)[None, :] < live_rows[:, None]).astype(jnp.float32)
    contrib = jnp.einsum("nrb,nbu->nru", leaf_y, update_blocks, precision=precise) * live_mask[:, None, :]
    flat_terms = jnp.transpose(contrib, (1, 0, 2)).reshape(VECS, NLEAVES * UPD)
    scattered = jnp.zeros((VECS, LEVELS * SEP_ORDER), jnp.float32).at[:, row_map.reshape(-1)].add(flat_terms)
    base_rows = sep_rhs.reshape(VECS, LEVELS, SEP_ORDER) - scattered.reshape(VECS, LEVELS, SEP_ORDER)
    diag_blocks = inv_diag.reshape(LEVELS, SEP_ORDER, SEP_ORDER)
    coupling = panels.reshape(NPAIRS, SEP_ORDER, SEP_ORDER)
    residuals = []
    y_list = []
    for level_now in range(LEVELS):
        current = base_rows[:, level_now]
        for lower_level in range(level_now):
            block_now = coupling[pair_index(level_now, lower_level, LEVELS)]
            current = current - jnp.dot(residuals[lower_level], block_now.T, precision=precise)
        residuals.append(current)
        y_list.append(jnp.dot(current, diag_blocks[level_now].T, precision=precise))
    solutions = [None] * LEVELS
    for level_now in range(LEVELS - 1, -1, -1):
        solved = jnp.dot(y_list[level_now], diag_blocks[level_now], precision=precise)
        for upper_level in range(level_now + 1, LEVELS):
            block_now = coupling[pair_index(upper_level, level_now, LEVELS)]
            solved = solved - jnp.dot(solutions[upper_level], block_now, precision=precise)
        solutions[level_now] = solved
    sep_solution = jnp.stack(solutions, axis=1)
    spread = sep_solution.reshape(VECS, LEVELS * SEP_ORDER)
    mapped = jnp.transpose(spread[:, row_map], (1, 0, 2)) * live_mask[:, None, :]
    reduced = leaf_y - jnp.einsum("nru,nbu->nrb", mapped, update_blocks, precision=precise)
    leaf_x = jnp.einsum("nrc,ncb->nrb", reduced, leaf_inv, precision=precise)
    return leaf_x, sep_solution.reshape(VECS, LEVELS, N_LEAF, N_SEP, SEG)
```

```python
import functools

import jax
import jax.numpy as jnp
from jax import lax
from jax.experimental import pallas as pl
from jax.experimental.pallas import tpu as pltpu
from jax.sharding import PartitionSpec as P

F32 = jnp.float32
BF16 = jnp.bfloat16
V = 16
LEVELS = 6
ROWS = 128
COLS = 1024
UPD = 1024
ALL = ("leaf", "sep")
VMEM_LIMIT = 40 * 1024 * 1024
NT = (((1,), (1,)), ((), ()))
NN = (((1,), (0,)), ((), ()))


def pair_index(upper, lower):
    return lower * (LEVELS - 1) - lower * (lower - 1) // 2 + upper - lower - 1


def iota(shape, dim):
    return lax.broadcasted_iota(jnp.int32, shape, dim)


def dot(a, b, dims):
    return lax.dot_general(a, b, dims, preferred_element_type=F32)


def split(x):
    high = x.astype(BF16)
    return high, (x - high.astype(F32)).astype(BF16)


def product(x, w, dims):
    xh, xl = split(x)
    wh, wl = split(w)
    m = x.shape[0]
    both = dot(jnp.concatenate([xh, xl], 0), wh, dims)
    return both[:m] + both[m:] + dot(xh, wl, dims)


def exact_rows(x, onehot, dims):
    xh, xl = split(x)
    m = x.shape[0]
    both = dot(jnp.concatenate([xh, xl], 0), onehot, dims)
    return both[:m] + both[m:]


def block_swap(t):
    gap = (iota((16, 128), 1) // 32 - iota((16, 128), 0) // 4) & 3
    out = t
    for d in range(1, 4):
        moved = pltpu.roll(pltpu.roll(t, 32 * d, 1), 16 - 4 * d, 0)
        out = jnp.where(gap == d, moved, out)
    return out


def call(body, out_shape, in_specs, out_specs, grid=(1,), scratch=(), aliases=None, flops=0, nbytes=0):
    return pl.pallas_call(
        body,
        out_shape=out_shape,
        grid=grid,
        in_specs=in_specs,
        out_specs=out_specs,
        scratch_shapes=scratch,
        input_output_aliases=aliases or {},
        compiler_params=pltpu.CompilerParams(vmem_limit_bytes=VMEM_LIMIT),
        cost_estimate=pl.CostEstimate(flops=flops, bytes_accessed=nbytes, transcendentals=0),
    )


def whole(shape):
    return pl.BlockSpec(shape, lambda *_: (0,) * len(shape))


def sds(shape, dtype=F32):
    return jax.ShapeDtypeStruct(shape, dtype)


SMEM = pl.BlockSpec(memory_space=pltpu.SMEM)


def leaf_forward(live_ref, rhs_ref, map_ref, inv_ref, upd_ref, y_ref, msg_ref, t_ref, rank_ref, acc):
    step = pl.program_id(0)

    @pl.when(step == 0)
    def _():
        acc[...] = jnp.zeros_like(acc)
        rows = map_ref[...]
        owner = (rows >> 5) & 127
        hot = (iota((128, UPD), 0) == owner).astype(F32)
        tri = (iota((UPD, UPD), 0) < iota((UPD, UPD), 1)).astype(F32).astype(BF16)
        before = dot(hot.astype(BF16), tri, NN)
        rank = jnp.sum(hot * before, axis=0, keepdims=True).astype(jnp.int32)
        rank_ref[...] = jnp.broadcast_to(rank, rank_ref.shape)
        for half in range(2):
            t_ref[pl.ds(128 * half, 128), :] = jnp.where((rank >> 3) == half, hot, 0.0).astype(BF16)

    y_part = product(rhs_ref[...], inv_ref[...], NT)
    y_ref[...] = y_part
    acc[...] += product(y_part, upd_ref[...], NN)

    @pl.when(step == pl.num_programs(0) - 1)
    def _():
        rows = map_ref[...]
        rank = rank_ref[0:1, :]
        live = iota((1, UPD), 1) < live_ref[0]
        group = iota((128, UPD), 0) >> 4
        spread = jnp.where((group == (rank & 7)) & live, jnp.concatenate([acc[...]] * 8, 0), 0.0)
        parts = jnp.concatenate(split(spread), 0)
        for half in range(2):
            got = dot(t_ref[pl.ds(128 * half, 128), :], parts, NT)
            msg_ref[pl.ds(half, 128, 4), :] = got[:, :128] + got[:, 128:]
        local = (rows >> 12) * 32 + (rows & 31) + 1
        places = jnp.where((iota((128, UPD), 0) == rank) & live, local.astype(F32), 0.0)
        hot = t_ref[pl.ds(0, 128), :].astype(F32) + t_ref[pl.ds(128, 128), :].astype(F32)
        msg_ref[pl.ds(2, 128, 4), :] = dot(hot.astype(BF16), places.astype(BF16), NT)
        msg_ref[pl.ds(3, 128, 4), :] = jnp.zeros((128, 128), F32)


def run_leaf_forward(live, rhs, rows, inv, upd):
    steps, part = 4, 256
    return call(
        leaf_forward,
        (sds((V, UPD)), sds((512, 128)), sds((256, UPD), BF16), sds((8, UPD), jnp.int32)),
        [
            SMEM,
            whole((V, 1024)),
            whole((1, UPD)),
            pl.BlockSpec((None, part, 1024), lambda i: (0, i, 0)),
            pl.BlockSpec((None, part, UPD), lambda i: (0, i, 0)),
        ],
        (pl.BlockSpec((V, part), lambda i: (0, i)), whole((512, 128)), whole((256, UPD)), whole((8, UPD))),
        grid=(steps,),
        scratch=[pltpu.VMEM((V, UPD), F32)],
        flops=2 * 16 * 3 * (2 << 20),
        nbytes=8 << 20,
    )(live, rhs, rows, inv, upd)


def leaf_backward(live_ref, got_ref, t_ref, rank_ref, y_ref, inv_ref, upd_ref, out_ref, mapped):
    step = pl.program_id(0)

    @pl.when(step == 0)
    def _():
        live = iota((1, UPD), 1) < live_ref[0]
        group = iota((128, UPD), 0) >> 4
        total = jnp.zeros((128, UPD), F32)
        for half in range(2):
            values = got_ref[pl.ds(half, 128, 2), :].T
            total += exact_rows(values, t_ref[pl.ds(128 * half, 128), :], NN)
        total = jnp.where((group == (rank_ref[0:1, :] & 7)) & live, total, 0.0)
        out = total[0:16]
        for g in range(1, 8):
            out += total[16 * g : 16 * g + 16]
        mapped[...] = out
        out_ref[...] = jnp.zeros_like(out_ref)

    z = y_ref[...] - product(mapped[...], upd_ref[...], NT)
    out_ref[...] += product(z, inv_ref[...], NN)


def run_leaf_backward(live, got, t, rank, y, inv, upd):
    steps, part = 4, 256
    return call(
        leaf_backward,
        sds((1, V, 1024)),
        [
            SMEM,
            whole((256, 128)),
            whole((256, UPD)),
            whole((8, UPD)),
            pl.BlockSpec((V, part), lambda i: (0, i)),
            pl.BlockSpec((None, part, 1024), lambda i: (0, i, 0)),
            pl.BlockSpec((None, part, UPD), lambda i: (0, i, 0)),
        ],
        pl.BlockSpec((None, V, 1024), lambda i: (0, 0, 0)),
        grid=(steps,),
        scratch=[pltpu.VMEM((V, UPD), F32)],
        flops=2 * 16 * 3 * (2 << 20),
        nbytes=8 << 20,
    )(live, got, t, rank, y, inv, upd)


def own_start(place_ref, got_ref, rhs_ref, pend_ref, msg_ref, index_ref):
    values = [got_ref[pl.ds(half, 128, 4), :].T for half in range(2)]
    index = got_ref[pl.ds(2, 128, 4), :]
    index_ref[...] = index
    column = (iota((128, 256), 1) + 1).astype(F32)
    total = jnp.zeros((V, 256), F32)
    for half in range(2):
        for g in range(8):
            j = 8 * half + g
            hot = jnp.where(index[:, j : j + 1] == column, 1.0, 0.0).astype(BF16)
            total += exact_rows(values[half][16 * g : 16 * g + 16], hot, NN)
    mine = iota((V, 128), 1) // 32 == place_ref[0]
    first = None
    for k in range(LEVELS):
        one = total[:, 32 * k : 32 * k + 32]
        row = jnp.where(mine, rhs_ref[:, 128 * k : 128 * k + 128] - jnp.concatenate([one] * 4, 1), 0.0)
        pend_ref[k] = row
        if k == 0:
            first = row
    turned = block_swap(first)
    chunk = turned[0:4] + turned[4:8] + turned[8:12] + turned[12:16]
    msg_ref[...] = jnp.concatenate([chunk] * 32, 0)


def run_own_start(place, got, rhs):
    return call(
        own_start,
        (sds((LEVELS, V, 128)), sds((128, 128)), sds((128, 128))),
        [SMEM, whole((512, 128)), whole((V, LEVELS * 128))],
        (whole((LEVELS, V, 128)), whole((128, 128)), whole((128, 128))),
        flops=1 << 27,
        nbytes=1 << 19,
    )(place, got, rhs)


def columns_of(got_ref, parts):
    total = got_ref[pl.ds(0, 128), :]
    for p in range(1, parts):
        total += got_ref[pl.ds(128 * p, 128), :]
    return jnp.concatenate([block_swap(total[16 * t : 16 * t + 16]) for t in range(8)], 1)


def row_message(msg_ref, rows):
    turned = block_swap(rows)
    for q in range(4):
        msg_ref[pl.ds(128 * q, 128), :] = jnp.concatenate([turned[4 * q : 4 * q + 4]] * 32, 0)


def forward_first(parts, got_ref, pend_ref, panel_ref, x_ref, msg_ref):
    x = columns_of(got_ref, parts)
    x_ref[...] = x
    row_message(msg_ref, pend_ref[...] - product(x, panel_ref[...].reshape(ROWS, COLS), NT))


def run_forward_first(k, parts, got, pend, panels):
    p = pair_index(k + 1, k)
    return call(
        functools.partial(forward_first, parts),
        (sds((V, COLS)), sds((512, 128))),
        [
            whole((128 * parts, 128)),
            pl.BlockSpec((None, V, 128), lambda i: (k + 1, 0, 0)),
            pl.BlockSpec((None, 4, None, 32, COLS), lambda i: (p, 0, 0, 0, 0)),
        ],
        (whole((V, COLS)), whole((512, 128))),
        flops=1 << 24,
        nbytes=1 << 20,
    )(got, pend, panels)


def forward_rest(x_ref, pend_ref, panel_ref, out_ref):
    out_ref[...] = pend_ref[...] - product(x_ref[...], panel_ref[...].reshape(ROWS, COLS), NT)


def run_forward_rest(k, x, pend, panels):
    first = pair_index(k + 2, k)
    count = LEVELS - 2 - k
    return call(
        forward_rest,
        sds((LEVELS, V, 128)),
        [
            whole((V, COLS)),
            pl.BlockSpec((None, V, 128), lambda i: (k + 2 + i, 0, 0)),
            pl.BlockSpec((None, 4, None, 32, COLS), lambda i: (first + i, 0, 0, 0, 0)),
        ],
        pl.BlockSpec((None, V, 128), lambda i: (k + 2 + i, 0, 0)),
        grid=(count,),
        aliases={1: 0},
        flops=count << 24,
        nbytes=count << 19,
    )(x, pend, panels)


def forward_diag(x_ref, diag_ref, y_ref):
    y_ref[...] = product(x_ref[...], diag_ref[...].reshape(ROWS, COLS), NT)


def diag_spec(k):
    return pl.BlockSpec((None, 4, None, 32, COLS), lambda i: (k, 0, 0, 0, 0))


def run_forward_diag(k, x, diag):
    return call(
        forward_diag,
        sds((V, 128)),
        [whole((V, COLS)), diag_spec(k)],
        whole((V, 128)),
        flops=1 << 24,
        nbytes=1 << 19,
    )(x, diag)


def forward_last(got_ref, y0, y1, y2, y3, y4, diag_ref, msg_ref):
    x = columns_of(got_ref, 4)
    last = product(x, diag_ref[...].reshape(ROWS, COLS), NT)
    for l in range(4):
        for k, one in enumerate((y0, y1, y2, y3, y4)):
            msg_ref[pl.ds(96 * l + 16 * k, 16), :] = one[...]
        msg_ref[pl.ds(96 * l + 80, 16), :] = last


def run_forward_last(got, ys, diag):
    return call(
        forward_last,
        sds((4 * 96, 128)),
        [whole((512, 128))] + [whole((V, 128))] * 5 + [diag_spec(5)],
        whole((4 * 96, 128)),
        flops=1 << 24,
        nbytes=1 << 20,
    )(got, *ys, diag)


def column_message(msg_ref, columns):
    for t in range(8):
        turned = block_swap(columns[:, 128 * t : 128 * t + 128])
        for l in range(4):
            msg_ref[pl.ds(128 * l + 16 * t, 16), :] = turned


def backward_start(got_ref, diag_ref, y_ref, msg_ref):
    y = got_ref[pl.ds(0, 96), :]
    for l in range(1, 4):
        y += got_ref[pl.ds(96 * l, 96), :]
    y_ref[...] = y
    column_message(msg_ref, product(y[80:96], diag_ref[...].reshape(ROWS, COLS), NN))


def run_backward_start(got, diag):
    return call(
        backward_start,
        (sds((96, 128)), sds((512, 128))),
        [whole((4 * 96, 128)), diag_spec(5)],
        (whole((96, 128)), whole((512, 128))),
        flops=1 << 24,
        nbytes=1 << 20,
    )(got, diag)


def backward_diag(y_ref, diag_ref, out_ref):
    out_ref[...] = product(y_ref[...], diag_ref[...].reshape(ROWS, COLS), NN)


def run_backward_diag(y, diag):
    return call(
        backward_diag,
        sds((LEVELS - 1, V, COLS)),
        [
            pl.BlockSpec((V, 128), lambda i: (i, 0)),
            pl.BlockSpec((None, 4, None, 32, COLS), lambda i: (i, 0, 0, 0, 0)),
        ],
        pl.BlockSpec((None, V, COLS), lambda i: (i, 0, 0)),
        grid=(LEVELS - 1,),
        flops=5 << 24,
        nbytes=5 << 19,
    )(y, diag)


def rows_of(got_ref):
    parts = []
    for q in range(4):
        total = got_ref[pl.ds(128 * q, 8), :]
        for t in range(1, 16):
            total += got_ref[pl.ds(128 * q + 8 * t, 8), :]
        parts.append(total[0:4] + total[4:8])
    return block_swap(jnp.concatenate(parts, 0))


def backward_first(got_ref, pend_ref, panel_ref, x_ref, msg_ref):
    x = rows_of(got_ref)
    x_ref[...] = x
    column_message(msg_ref, pend_ref[...] - product(x, panel_ref[...].reshape(ROWS, COLS), NN))


def run_backward_first(k, got, pend, panels):
    p = pair_index(k, k - 1)
    return call(
        backward_first,
        (sds((V, 128)), sds((512, 128))),
        [
            whole((512, 128)),
            pl.BlockSpec((None, V, COLS), lambda i: (k - 1, 0, 0)),
            pl.BlockSpec((None, 4, None, 32, COLS), lambda i: (p, 0, 0, 0, 0)),
        ],
        (whole((V, 128)), whole((512, 128))),
        flops=1 << 24,
        nbytes=1 << 20,
    )(got, pend, panels)


def backward_rest(x_ref, pend_ref, panel_ref, out_ref):
    out_ref[...] = pend_ref[...] - product(x_ref[...], panel_ref[...].reshape(ROWS, COLS), NN)


def run_backward_rest(k, x, pend, panels):
    count = k - 1
    return call(
        backward_rest,
        sds((LEVELS - 1, V, COLS)),
        [
            whole((V, 128)),
            pl.BlockSpec((None, V, COLS), lambda i: (i, 0, 0)),
            pl.BlockSpec((None, 4, None, 32, COLS), lambda i: (pair_index(k, i), 0, 0, 0, 0)),
        ],
        pl.BlockSpec((None, V, COLS), lambda i: (i, 0, 0)),
        grid=(count,),
        aliases={1: 0},
        flops=count << 24,
        nbytes=count << 19,
    )(x, pend, panels)


def own_finish(place_ref, got_ref, x1, x2, x3, x4, x5, index_ref, x_ref, msg_ref):
    x0 = rows_of(got_ref)
    levels = [x0] + [r[...] for r in (x1, x2, x3, x4, x5)]
    mine = []
    for k, x in enumerate(levels):
        x_ref[k] = x
        one = jnp.zeros((V, 32), F32)
        for q in range(4):
            one = jnp.where(place_ref[0] == q, x[:, 32 * q : 32 * q + 32], one)
        mine.append(one)
    rows = jnp.concatenate(mine + [jnp.zeros((V, 64), F32)], 1)
    high, low = split(jnp.concatenate([rows] * 8, 0))
    table = jnp.concatenate([high, low], 0)
    index = index_ref[...]
    column = (iota((128, 256), 1) + 1).astype(F32)
    group = iota((128, 128), 1) >> 4
    for half in range(2):
        out = jnp.zeros((128, 128), F32)
        for g in range(8):
            j = 8 * half + g
            hot = jnp.where(index[:, j : j + 1] == column, 1.0, 0.0).astype(BF16)
            got = dot(hot, table, NT)
            out = jnp.where(group == g, got[:, :128] + got[:, 128:], out)
        msg_ref[pl.ds(half, 128, 2), :] = out


def run_own_finish(place, got, xs, index):
    return call(
        own_finish,
        (sds((LEVELS, V, 128)), sds((256, 128))),
        [SMEM, whole((512, 128))] + [whole((V, 128))] * 5 + [whole((128, 128))],
        (whole((LEVELS, V, 128)), whole((256, 128))),
        flops=1 << 27,
        nbytes=1 << 20,
    )(place, got, *xs, index)


def exchange(message, axis=ALL):
    return lax.all_to_all(message, axis, 0, 0, tiled=True)


def per_device(leaf_rhs, leaf_inv, update_blocks, row_map, live_rows, sep_rhs, inv_diag, panels):
    place = lax.axis_index("leaf").astype(jnp.int32).reshape(1)
    rhs = sep_rhs.reshape(V, LEVELS * 128)
    leaf_y, message, table, rank = run_leaf_forward(live_rows, leaf_rhs[0], row_map, leaf_inv, update_blocks)
    pend, message, index = run_own_start(place, exchange(message), rhs)
    got, parts = exchange(message, "sep"), 1
    ys = []
    for k in range(LEVELS - 1):
        x, message = run_forward_first(k, parts, got, pend, panels)
        got, parts = exchange(message), 4
        if k + 2 < LEVELS:
            pend = run_forward_rest(k, x, pend, panels)
        ys.append(run_forward_diag(k, x, inv_diag))
    message = run_forward_last(got, ys, inv_diag)
    y, message = run_backward_start(exchange(message, "leaf"), inv_diag)
    got = exchange(message)
    pend = run_backward_diag(y, inv_diag)
    xs = []
    for k in range(LEVELS - 1, 0, -1):
        x, message = run_backward_first(k, got, pend, panels)
        xs.insert(0, x)
        got = exchange(message)
        if k > 1:
            pend = run_backward_rest(k, x, pend, panels)
    levels, message = run_own_finish(place, got, xs, index)
    got = exchange(message)
    leaf_x = run_leaf_backward(live_rows, got, table, rank, leaf_y, leaf_inv, update_blocks)
    sep_solution = levels.reshape(LEVELS, V, 4, 1, 32).transpose(1, 0, 2, 3, 4)
    return leaf_x, sep_solution


def solution(mesh):
    in_specs = (
        P(ALL, None, None),
        P(ALL, None, None),
        P(ALL, None, None),
        P(ALL, None),
        P(ALL),
        P(None, None, None, "sep", None),
        P(None, None, "sep", None, "leaf"),
        P(None, None, "sep", None, "leaf"),
    )
    out_specs = (P(ALL, None, None), P(None, None, None, "sep", None))
    return jax.shard_map(per_device, mesh=mesh, in_specs=in_specs, out_specs=out_specs, check_vma=False)
```

```python
import functools

import jax
import jax.numpy as jnp
from jax import lax
from jax.experimental import pallas as pl
from jax.experimental.pallas import tpu as pltpu
from jax.sharding import PartitionSpec as P

F32 = jnp.float32
BF16 = jnp.bfloat16
V = 16
LEVELS = 6
ROWS = 128
COLS = 1024
UPD = 1024
ALL = ("leaf", "sep")
VMEM_LIMIT = 52 * 1024 * 1024
NT = (((1,), (1,)), ((), ()))
NN = (((1,), (0,)), ((), ()))


def pair_index(upper, lower):
    return lower * (LEVELS - 1) - lower * (lower - 1) // 2 + upper - lower - 1


def iota(shape, dim):
    return lax.broadcasted_iota(jnp.int32, shape, dim)


def dot(a, b, dims):
    return lax.dot_general(a, b, dims, preferred_element_type=F32)


def split(x):
    high = x.astype(BF16)
    return high, (x - high.astype(F32)).astype(BF16)


def product(x, w, dims):
    xh, xl = split(x)
    wh, wl = split(w)
    m = x.shape[0]
    both = dot(jnp.concatenate([xh, xl], 0), wh, dims)
    return both[:m] + both[m:] + dot(xh, wl, dims)


def exact_rows(x, onehot, dims):
    xh, xl = split(x)
    m = x.shape[0]
    both = dot(jnp.concatenate([xh, xl], 0), onehot, dims)
    return both[:m] + both[m:]


def block_swap(t):
    gap = (iota((16, 128), 1) // 32 - iota((16, 128), 0) // 4) & 3
    out = t
    for d in range(1, 4):
        moved = pltpu.roll(pltpu.roll(t, 32 * d, 1), 16 - 4 * d, 0)
        out = jnp.where(gap == d, moved, out)
    return out


def call(body, out_shape, in_specs, out_specs, scratch=(), flops=0, nbytes=0, limit=VMEM_LIMIT):
    return pl.pallas_call(
        body,
        out_shape=out_shape,
        in_specs=in_specs,
        out_specs=out_specs,
        scratch_shapes=scratch,
        compiler_params=pltpu.CompilerParams(vmem_limit_bytes=limit),
        cost_estimate=pl.CostEstimate(flops=flops, bytes_accessed=nbytes, transcendentals=0),
    )


def sds(shape, dtype=F32):
    return jax.ShapeDtypeStruct(shape, dtype)


VM = pl.BlockSpec(memory_space=pltpu.VMEM)
SMEM = pl.BlockSpec(memory_space=pltpu.SMEM)
HBM = pl.BlockSpec(memory_space=pltpu.HBM)


def fetch(sources, buffer, sems):
    copies = [pltpu.make_async_copy(src, buffer.at[n], sems.at[n]) for n, src in enumerate(sources)]
    for one in copies:
        one.start()
    return copies


def leaf_forward(live_ref, rhs_hbm, map_hbm, inv_ref, upd_ref, y_ref, msg_ref, t_ref, rank_ref, rhs_ref, map_ref, buffer, sems):
    step = UPD // 4
    small = [pltpu.make_async_copy(map_hbm, map_ref, sems.at[8]), pltpu.make_async_copy(rhs_hbm, rhs_ref, sems.at[9])]
    for one in small:
        one.start()
    sources = []
    for n in range(4):
        for ref in (inv_ref, upd_ref):
            sources.append(ref.at[0, pl.ds(step * n, step), :])
    copies = fetch(sources, buffer, sems)
    small[0].wait()
    rows = map_ref[...]
    owner = (rows >> 5) & 127
    hot = (iota((128, UPD), 0) == owner).astype(F32)
    ones = jnp.where((iota((128, 256), 0) < iota((128, 256), 1)), 1.0, 0.0).astype(BF16)
    carry = jnp.zeros((128, 128), F32)
    before = []
    for n in range(UPD // 128):
        counts = dot(hot[:, 128 * n : 128 * n + 128].astype(BF16), ones, NN)
        before.append(counts[:, :128] + carry)
        carry += counts[:, 128:]
    before = jnp.concatenate(before, 1)
    rank = jnp.sum(hot * before, axis=0, keepdims=True).astype(jnp.int32)
    rank_ref[...] = jnp.broadcast_to(rank, rank_ref.shape)
    for half in range(2):
        t_ref[pl.ds(128 * half, 128), :] = jnp.where((rank >> 3) == half, hot, 0.0).astype(BF16)
    live = iota((1, UPD), 1) < live_ref[0]
    local = (rows >> 12) * 32 + (rows & 31) + 1
    places = jnp.where((iota((128, UPD), 0) == rank) & live, local.astype(F32), 0.0)
    msg_ref[pl.ds(2, 128, 4), :] = dot(hot.astype(BF16), places.astype(BF16), NT)
    msg_ref[pl.ds(3, 128, 4), :] = jnp.zeros((128, 128), F32)
    acc = jnp.zeros((V, UPD), F32)
    small[1].wait()
    for n in range(4):
        copies[2 * n].wait()
        y_part = product(rhs_ref[0], buffer[2 * n], NT)
        y_ref[:, step * n : step * n + step] = y_part
        copies[2 * n + 1].wait()
        acc += product(y_part, buffer[2 * n + 1], NN)
    group = iota((128, UPD), 0) >> 4
    spread = jnp.where((group == (rank & 7)) & live, jnp.concatenate([acc] * 8, 0), 0.0)
    parts = jnp.concatenate(split(spread), 0)
    for half in range(2):
        got = dot(t_ref[pl.ds(128 * half, 128), :], parts, NT)
        msg_ref[pl.ds(half, 128, 4), :] = got[:, :128] + got[:, 128:]


def run_leaf_forward(live, rhs, rows, inv, upd):
    return call(
        leaf_forward,
        (sds((V, UPD)), sds((512, 128)), sds((256, UPD), BF16), sds((8, UPD), jnp.int32)),
        [SMEM, HBM, HBM, HBM, HBM],
        (VM, VM, VM, VM),
        scratch=[
            pltpu.VMEM((1, V, 1024), F32),
            pltpu.VMEM((1, UPD), jnp.int32),
            pltpu.VMEM((8, UPD // 4, 1024), F32),
            pltpu.SemaphoreType.DMA((10,)),
        ],
        flops=2 * 16 * 3 * (2 << 20),
        nbytes=8 << 20,
        limit=60 * 1024 * 1024,
    )(live, rhs, rows, inv, upd)


def leaf_backward(live_ref, got_ref, t_ref, rank_ref, y_ref, inv_ref, upd_ref, out_ref, buffer, sems):
    step = UPD // 4
    sources = []
    for n in range(4):
        for ref in (upd_ref, inv_ref):
            sources.append(ref.at[0, pl.ds(step * n, step), :])
    copies = fetch(sources, buffer, sems)
    live = iota((1, UPD), 1) < live_ref[0]
    group = iota((128, UPD), 0) >> 4
    total = jnp.zeros((128, UPD), F32)
    for half in range(2):
        values = got_ref[pl.ds(half, 128, 2), :].T
        total += exact_rows(values, t_ref[pl.ds(128 * half, 128), :], NN)
    total = jnp.where((group == (rank_ref[0:1, :] & 7)) & live, total, 0.0)
    mapped = total[0:16]
    for g in range(1, 8):
        mapped += total[16 * g : 16 * g + 16]
    out = jnp.zeros((V, 1024), F32)
    for n in range(4):
        copies[2 * n].wait()
        z = y_ref[:, step * n : step * n + step] - product(mapped, buffer[2 * n], NT)
        copies[2 * n + 1].wait()
        out += product(z, buffer[2 * n + 1], NN)
    out_ref[0] = out


def run_leaf_backward(live, got, t, rank, y, inv, upd):
    return call(
        leaf_backward,
        sds((1, V, 1024)),
        [SMEM, VM, VM, VM, VM, HBM, HBM],
        VM,
        scratch=[pltpu.VMEM((8, UPD // 4, 1024), F32), pltpu.SemaphoreType.DMA((8,))],
        flops=2 * 16 * 3 * (2 << 20),
        nbytes=8 << 20,
    )(live, got, t, rank, y, inv, upd)


def own_start(place_ref, got_ref, rhs_ref, pend_ref, msg_ref, index_ref):
    values = [got_ref[pl.ds(half, 128, 4), :].T for half in range(2)]
    index = got_ref[pl.ds(2, 128, 4), :]
    index_ref[...] = index
    column = (iota((128, 256), 1) + 1).astype(F32)
    total = jnp.zeros((V, 256), F32)
    for half in range(2):
        for g in range(8):
            j = 8 * half + g
            hot = jnp.where(index[:, j : j + 1] == column, 1.0, 0.0).astype(BF16)
            total += exact_rows(values[half][16 * g : 16 * g + 16], hot, NN)
    mine = iota((V, 128), 1) // 32 == place_ref[0]
    first = None
    for k in range(LEVELS):
        one = total[:, 32 * k : 32 * k + 32]
        row = jnp.where(mine, rhs_ref[:, 128 * k : 128 * k + 128] - jnp.concatenate([one] * 4, 1), 0.0)
        pend_ref[k] = row
        if k == 0:
            first = row
    turned = block_swap(first)
    chunk = turned[0:4] + turned[4:8] + turned[8:12] + turned[12:16]
    msg_ref[...] = jnp.concatenate([chunk] * 32, 0)


def run_own_start(place, got, rhs):
    return call(
        own_start,
        (sds((LEVELS, V, 128)), sds((128, 128)), sds((128, 128))),
        [SMEM, VM, VM],
        (VM, VM, VM),
        flops=1 << 27,
        nbytes=1 << 19,
    )(place, got, rhs)


def columns_of(got_ref, parts):
    total = got_ref[pl.ds(0, 128), :]
    for p in range(1, parts):
        total += got_ref[pl.ds(128 * p, 128), :]
    return jnp.concatenate([block_swap(total[16 * t : 16 * t + 16]) for t in range(8)], 1)


def row_message(msg_ref, rows):
    turned = block_swap(rows)
    for q in range(4):
        msg_ref[pl.ds(128 * q, 128), :] = jnp.concatenate([turned[4 * q : 4 * q + 4]] * 32, 0)


def block_parts(block):
    return jnp.concatenate(split(block.reshape(ROWS, COLS)), 0)


def times_columns(x, w):
    out = dot(jnp.concatenate(split(x), 0), w, NT)
    return (out[:V, :ROWS] + out[V:, :ROWS]) + (out[:V, ROWS:] + out[V:, ROWS:])


def times_rows(x, w):
    half = jnp.concatenate(split(x), 0)
    out = dot(jnp.concatenate([half, half], 1), w, NN)
    return out[:V] + out[V:]


PARTS = (2 * ROWS, COLS)


def first_block(panels_ref, w_ref, buffer, sems):
    fetch([panels_ref.at[pair_index(1, 0), :, 0]], buffer, sems)[0].wait()
    w_ref[...] = block_parts(buffer[0])


def buffers(count):
    return [pltpu.VMEM((count, 4, 32, COLS), F32), pltpu.SemaphoreType.DMA((count,))]


def run_first_block(panels):
    return call(first_block, sds(PARTS, BF16), [HBM], VM, scratch=buffers(1), flops=1 << 20, nbytes=1 << 20)(panels)


def forward_first(k, parts, got_ref, pend_ref, w_ref, x_ref, msg_ref):
    x = columns_of(got_ref, parts)
    x_ref[...] = x
    row_message(msg_ref, pend_ref[k + 1] - times_columns(x, w_ref[...]))


def run_forward_first(k, parts, got, pend, w):
    return call(
        functools.partial(forward_first, k, parts),
        (sds((V, COLS)), sds((512, 128))),
        [VM, VM, VM],
        (VM, VM),
        flops=1 << 24,
        nbytes=1 << 20,
    )(got, pend, w)


def forward_rest(k, x_ref, pend_ref, panels_ref, diag_ref, out_ref, y_ref, w_ref, buffer, sems):
    later = range(k + 2, LEVELS)
    sources = [panels_ref.at[pair_index(j, k), :, 0] for j in later] + [diag_ref.at[k, :, 0]]
    sources.append(panels_ref.at[pair_index(k + 2, k + 1), :, 0] if k + 2 < LEVELS else diag_ref.at[k + 1, :, 0])
    copies = fetch(sources, buffer, sems)
    x = x_ref[...]
    out_ref[...] = pend_ref[...]
    for n, j in enumerate(later):
        copies[n].wait()
        out_ref[j] = pend_ref[j] - times_columns(x, block_parts(buffer[n]))
    copies[-2].wait()
    y_ref[...] = times_columns(x, block_parts(buffer[len(sources) - 2]))
    copies[-1].wait()
    w_ref[...] = block_parts(buffer[len(sources) - 1])


def run_forward_rest(k, x, pend, panels, diag):
    count = LEVELS - k
    return call(
        functools.partial(forward_rest, k),
        (sds((LEVELS, V, 128)), sds((V, 128)), sds(PARTS, BF16)),
        [VM, VM, HBM, HBM],
        (VM, VM, VM),
        scratch=buffers(count),
        flops=count << 24,
        nbytes=count << 19,
    )(x, pend, panels, diag)


def forward_last(got_ref, y0, y1, y2, y3, y4, w_ref, msg_ref):
    x = columns_of(got_ref, 4)
    last = times_columns(x, w_ref[...])
    for l in range(4):
        for k, one in enumerate((y0, y1, y2, y3, y4)):
            msg_ref[pl.ds(96 * l + 16 * k, 16), :] = one[...]
        msg_ref[pl.ds(96 * l + 80, 16), :] = last


def run_forward_last(got, ys, w):
    return call(
        forward_last,
        sds((4 * 96, 128)),
        [VM] + [VM] * 5 + [VM],
        VM,
        flops=1 << 24,
        nbytes=1 << 20,
    )(got, *ys, w)


def column_message(msg_ref, columns):
    for t in range(8):
        turned = block_swap(columns[:, 128 * t : 128 * t + 128])
        for l in range(4):
            msg_ref[pl.ds(128 * l + 16 * t, 16), :] = turned


def backward_start(got_ref, w_ref, y_ref, msg_ref):
    y = got_ref[pl.ds(0, 96), :]
    for l in range(1, 4):
        y += got_ref[pl.ds(96 * l, 96), :]
    y_ref[...] = y
    column_message(msg_ref, times_rows(y[80:96], w_ref[...]))


def run_backward_start(got, w):
    return call(
        backward_start,
        (sds((96, 128)), sds((512, 128))),
        [VM, VM],
        (VM, VM),
        flops=1 << 24,
        nbytes=1 << 20,
    )(got, w)


def backward_diag(y_ref, panels_ref, diag_ref, out_ref, w_ref, buffer, sems):
    count = LEVELS - 1
    sources = [diag_ref.at[k, :, 0] for k in range(count)] + [panels_ref.at[pair_index(count, count - 1), :, 0]]
    copies = fetch(sources, buffer, sems)
    for k in range(count):
        copies[k].wait()
        out_ref[k] = times_rows(y_ref[pl.ds(16 * k, 16), :], block_parts(buffer[k]))
    copies[count].wait()
    w_ref[...] = block_parts(buffer[count])


def run_backward_diag(y, panels, diag):
    return call(
        backward_diag,
        (sds((LEVELS - 1, V, COLS)), sds(PARTS, BF16)),
        [VM, HBM, HBM],
        (VM, VM),
        scratch=buffers(LEVELS),
        flops=5 << 24,
        nbytes=3 << 20,
    )(y, panels, diag)


def rows_of(got_ref):
    parts = []
    for q in range(4):
        total = got_ref[pl.ds(128 * q, 8), :]
        for t in range(1, 16):
            total += got_ref[pl.ds(128 * q + 8 * t, 8), :]
        parts.append(total[0:4] + total[4:8])
    return block_swap(jnp.concatenate(parts, 0))


def backward_first(k, got_ref, pend_ref, w_ref, x_ref, msg_ref):
    x = rows_of(got_ref)
    x_ref[...] = x
    column_message(msg_ref, pend_ref[k - 1] - times_rows(x, w_ref[...]))


def run_backward_first(k, got, pend, w):
    return call(
        functools.partial(backward_first, k),
        (sds((V, 128)), sds((512, 128))),
        [VM, VM, VM],
        (VM, VM),
        flops=1 << 24,
        nbytes=1 << 20,
    )(got, pend, w)


def backward_rest(k, x_ref, pend_ref, panels_ref, out_ref, w_ref, buffer, sems):
    count = k - 1
    sources = [panels_ref.at[pair_index(k, j), :, 0] for j in range(count)]
    sources.append(panels_ref.at[pair_index(k - 1, k - 2), :, 0])
    copies = fetch(sources, buffer, sems)
    x = x_ref[...]
    for j in range(count):
        copies[j].wait()
        out_ref[j] = pend_ref[j] - times_rows(x, block_parts(buffer[j]))
    copies[count].wait()
    w_ref[...] = block_parts(buffer[count])


def run_backward_rest(k, x, pend, panels):
    count = k - 1
    return call(
        functools.partial(backward_rest, k),
        (sds((count, V, COLS)), sds(PARTS, BF16)),
        [VM, VM, HBM],
        (VM, VM),
        scratch=buffers(count + 1),
        flops=count << 24,
        nbytes=count << 19,
    )(x, pend, panels)


def own_finish(place_ref, got_ref, x1, x2, x3, x4, x5, index_ref, x_ref, msg_ref):
    x0 = rows_of(got_ref)
    levels = [x0] + [r[...] for r in (x1, x2, x3, x4, x5)]
    mine = []
    for k, x in enumerate(levels):
        x_ref[k] = x
        one = jnp.zeros((V, 32), F32)
        for q in range(4):
            one = jnp.where(place_ref[0] == q, x[:, 32 * q : 32 * q + 32], one)
        mine.append(one)
    rows = jnp.concatenate(mine + [jnp.zeros((V, 64), F32)], 1)
    high, low = split(jnp.concatenate([rows] * 8, 0))
    table = jnp.concatenate([high, low], 0)
    index = index_ref[...]
    column = (iota((128, 256), 1) + 1).astype(F32)
    group = iota((128, 128), 1) >> 4
    for half in range(2):
        out = jnp.zeros((128, 128), F32)
        for g in range(8):
            j = 8 * half + g
            hot = jnp.where(index[:, j : j + 1] == column, 1.0, 0.0).astype(BF16)
            got = dot(hot, table, NT)
            out = jnp.where(group == g, got[:, :128] + got[:, 128:], out)
        msg_ref[pl.ds(half, 128, 2), :] = out


def run_own_finish(place, got, xs, index):
    return call(
        own_finish,
        (sds((LEVELS, V, 128)), sds((256, 128))),
        [SMEM, VM] + [VM] * 5 + [VM],
        (VM, VM),
        flops=1 << 27,
        nbytes=1 << 20,
    )(place, got, *xs, index)


def exchange(message, axis=ALL):
    return lax.all_to_all(message, axis, 0, 0, tiled=True)


def per_device(leaf_rhs, leaf_inv, update_blocks, row_map, live_rows, sep_rhs, inv_diag, panels):
    place = lax.axis_index("leaf").astype(jnp.int32).reshape(1)
    rhs = sep_rhs.reshape(V, LEVELS * 128)
    leaf_y, message, table, rank = run_leaf_forward(live_rows, leaf_rhs, row_map, leaf_inv, update_blocks)
    pend, message, index = run_own_start(place, exchange(message), rhs)
    got, parts = exchange(message, "sep"), 1
    w = run_first_block(panels)
    ys = []
    for k in range(LEVELS - 1):
        x, message = run_forward_first(k, parts, got, pend, w)
        got, parts = exchange(message), 4
        pend, y, w = run_forward_rest(k, x, pend, panels, inv_diag)
        ys.append(y)
    y, message = run_backward_start(exchange(run_forward_last(got, ys, w), "leaf"), w)
    got = exchange(message)
    pend, w = run_backward_diag(y, panels, inv_diag)
    xs = []
    for k in range(LEVELS - 1, 0, -1):
        x, message = run_backward_first(k, got, pend, w)
        xs.insert(0, x)
        got = exchange(message)
        if k > 1:
            pend, w = run_backward_rest(k, x, pend, panels)
    levels, message = run_own_finish(place, got, xs, index)
    got = exchange(message)
    leaf_x = run_leaf_backward(live_rows, got, table, rank, leaf_y, leaf_inv, update_blocks)
    sep_solution = levels.reshape(LEVELS, V, 4, 1, 32).transpose(1, 0, 2, 3, 4)
    return leaf_x, sep_solution


def solution(mesh):
    in_specs = (
        P(ALL, None, None),
        P(ALL, None, None),
        P(ALL, None, None),
        P(ALL, None),
        P(ALL),
        P(None, None, None, "sep", None),
        P(None, None, "sep", None, "leaf"),
        P(None, None, "sep", None, "leaf"),
    )
    out_specs = (P(ALL, None, None), P(None, None, None, "sep", None))
    return jax.shard_map(per_device, mesh=mesh, in_specs=in_specs, out_specs=out_specs, check_vma=False)
```

```python
import functools

import jax
import jax.numpy as jnp
from jax import lax
from jax.experimental import pallas as pl
from jax.experimental.pallas import tpu as pltpu
from jax.sharding import PartitionSpec as P

F32 = jnp.float32
BF16 = jnp.bfloat16
V = 16
LEVELS = 6
ROWS = 128
COLS = 1024
UPD = 1024
CHUNKS = 2
ALL = ("leaf", "sep")
VMEM_LIMIT = 51 * 1024 * 1024
NT = (((1,), (1,)), ((), ()))
NN = (((1,), (0,)), ((), ()))


def pair_index(upper, lower):
    return lower * (LEVELS - 1) - lower * (lower - 1) // 2 + upper - lower - 1


def iota(shape, dim):
    return lax.broadcasted_iota(jnp.int32, shape, dim)


def dot(a, b, dims):
    return lax.dot_general(a, b, dims, preferred_element_type=F32)


def split(x):
    high = x.astype(BF16)
    return high, (x - high.astype(F32)).astype(BF16)


def product(x, w, dims):
    xh, xl = split(x)
    wh, wl = split(w)
    m = x.shape[0]
    both = dot(jnp.concatenate([xh, xl], 0), wh, dims)
    return both[:m] + both[m:] + dot(xh, wl, dims)


def exact_rows(x, onehot, dims):
    xh, xl = split(x)
    m = x.shape[0]
    both = dot(jnp.concatenate([xh, xl], 0), onehot, dims)
    return both[:m] + both[m:]


def block_swap(t):
    gap = (iota((16, 128), 1) // 32 - iota((16, 128), 0) // 4) & 3
    out = t
    for d in range(1, 4):
        moved = pltpu.roll(pltpu.roll(t, 32 * d, 1), 16 - 4 * d, 0)
        out = jnp.where(gap == d, moved, out)
    return out


def call(body, out_shape, in_specs, out_specs, scratch=(), flops=0, nbytes=0, limit=VMEM_LIMIT):
    return pl.pallas_call(
        body,
        out_shape=out_shape,
        in_specs=in_specs,
        out_specs=out_specs,
        scratch_shapes=scratch,
        compiler_params=pltpu.CompilerParams(vmem_limit_bytes=limit),
        cost_estimate=pl.CostEstimate(flops=flops, bytes_accessed=nbytes, transcendentals=0),
    )


def sds(shape, dtype=F32):
    return jax.ShapeDtypeStruct(shape, dtype)


VM = pl.BlockSpec(memory_space=pltpu.VMEM)
SMEM = pl.BlockSpec(memory_space=pltpu.SMEM)
ANY = pl.BlockSpec(memory_space=pl.ANY)
HBM = pl.BlockSpec(memory_space=pltpu.HBM)


def fetch(sources, buffer, sems):
    copies = [pltpu.make_async_copy(src, buffer.at[n], sems.at[n]) for n, src in enumerate(sources)]
    for one in copies:
        one.start()
    return copies


def leaf_forward(live_ref, rhs_hbm, map_hbm, inv_ref, upd_ref, y_ref, msg_ref, t_ref, rank_ref, rhs_ref, map_ref, buffer, sems):
    step = UPD // CHUNKS
    small = [pltpu.make_async_copy(map_hbm, map_ref, sems.at[2 * CHUNKS]), pltpu.make_async_copy(rhs_hbm, rhs_ref, sems.at[2 * CHUNKS + 1])]
    for one in small:
        one.start()
    sources = []
    for n in range(CHUNKS):
        for ref in (inv_ref, upd_ref):
            sources.append(ref.at[0, pl.ds(step * n, step), :])
    copies = fetch(sources, buffer, sems)
    small[0].wait()
    rows = map_ref[...]
    owner = (rows >> 5) & 127
    hot = (iota((128, UPD), 0) == owner).astype(F32)
    ones = jnp.where((iota((128, 256), 0) < iota((128, 256), 1)), 1.0, 0.0).astype(BF16)
    carry = jnp.zeros((128, 128), F32)
    before = []
    for n in range(UPD // 128):
        counts = dot(hot[:, 128 * n : 128 * n + 128].astype(BF16), ones, NN)
        before.append(counts[:, :128] + carry)
        carry += counts[:, 128:]
    before = jnp.concatenate(before, 1)
    rank = jnp.sum(hot * before, axis=0, keepdims=True).astype(jnp.int32)
    rank_ref[...] = jnp.broadcast_to(rank, rank_ref.shape)
    for half in range(2):
        t_ref[pl.ds(128 * half, 128), :] = jnp.where((rank >> 3) == half, hot, 0.0).astype(BF16)
    live = iota((1, UPD), 1) < live_ref[0]
    local = (rows >> 12) * 32 + (rows & 31) + 1
    places = jnp.where((iota((128, UPD), 0) == rank) & live, local.astype(F32), 0.0)
    msg_ref[pl.ds(2, 128, 4), :] = dot(hot.astype(BF16), places.astype(BF16), NT)
    msg_ref[pl.ds(3, 128, 4), :] = jnp.zeros((128, 128), F32)
    acc = jnp.zeros((V, UPD), F32)
    small[1].wait()
    for n in range(CHUNKS):
        copies[2 * n].wait()
        y_part = product(rhs_ref[0], buffer[2 * n], NT)
        y_ref[:, step * n : step * n + step] = y_part
        copies[2 * n + 1].wait()
        acc += product(y_part, buffer[2 * n + 1], NN)
    group = iota((128, UPD), 0) >> 4
    spread = jnp.where((group == (rank & 7)) & live, jnp.concatenate([acc] * 8, 0), 0.0)
    parts = jnp.concatenate(split(spread), 0)
    for half in range(2):
        got = dot(t_ref[pl.ds(128 * half, 128), :], parts, NT)
        msg_ref[pl.ds(half, 128, 4), :] = got[:, :128] + got[:, 128:]


def run_leaf_forward(live, rhs, rows, inv, upd):
    return call(
        leaf_forward,
        (sds((V, UPD)), sds((512, 128)), sds((256, UPD), BF16), sds((8, UPD), jnp.int32)),
        [SMEM, HBM, HBM, HBM, HBM],
        (VM, VM, VM, VM),
        scratch=[
            pltpu.VMEM((1, V, 1024), F32),
            pltpu.VMEM((1, UPD), jnp.int32),
            pltpu.VMEM((2 * CHUNKS, UPD // CHUNKS, 1024), F32),
            pltpu.SemaphoreType.DMA((2 * CHUNKS + 2,)),
        ],
        flops=2 * 16 * 3 * (2 << 20),
        nbytes=8 << 20,
        limit=60 * 1024 * 1024,
    )(live, rhs, rows, inv, upd)


def leaf_backward(live_ref, got_ref, t_ref, rank_ref, y_ref, inv_ref, upd_ref, out_ref, buffer, sems):
    step = UPD // CHUNKS
    sources = []
    for n in range(CHUNKS):
        for ref in (upd_ref, inv_ref):
            sources.append(ref.at[0, pl.ds(step * n, step), :])
    copies = fetch(sources, buffer, sems)
    live = iota((1, UPD), 1) < live_ref[0]
    group = iota((128, UPD), 0) >> 4
    total = jnp.zeros((128, UPD), F32)
    for half in range(2):
        values = got_ref[pl.ds(half, 128, 2), :].T
        total += exact_rows(values, t_ref[pl.ds(128 * half, 128), :], NN)
    total = jnp.where((group == (rank_ref[0:1, :] & 7)) & live, total, 0.0)
    mapped = total[0:16]
    for g in range(1, 8):
        mapped += total[16 * g : 16 * g + 16]
    out = jnp.zeros((V, 1024), F32)
    for n in range(CHUNKS):
        copies[2 * n].wait()
        z = y_ref[:, step * n : step * n + step] - product(mapped, buffer[2 * n], NT)
        copies[2 * n + 1].wait()
        out += product(z, buffer[2 * n + 1], NN)
    out_ref[0] = out


def run_leaf_backward(live, got, t, rank, y, inv, upd):
    return call(
        leaf_backward,
        sds((1, V, 1024)),
        [SMEM, VM, VM, VM, VM, HBM, HBM],
        VM,
        scratch=[pltpu.VMEM((2 * CHUNKS, UPD // CHUNKS, 1024), F32), pltpu.SemaphoreType.DMA((2 * CHUNKS,))],
        flops=2 * 16 * 3 * (2 << 20),
        nbytes=8 << 20,
    )(live, got, t, rank, y, inv, upd)


def own_start(place_ref, got_ref, rhs_ref, after_ref, pend_ref, msg_ref, index_ref):
    values = [got_ref[pl.ds(half, 128, 4), :].T for half in range(2)]
    index = got_ref[pl.ds(2, 128, 4), :]
    index_ref[...] = index
    column = (iota((128, 256), 1) + 1).astype(F32)
    hot, rows = [], []
    for half in range(2):
        for g in range(8):
            j = 8 * half + g
            hot.append(jnp.where(index[:, j : j + 1] == column, 1.0, 0.0).astype(BF16))
            rows.append(values[half][16 * g : 16 * g + 16])
    total = exact_rows(jnp.concatenate(rows, 1), jnp.concatenate(hot, 0), NN)
    mine = iota((V, 128), 1) // 32 == place_ref[0]
    first = None
    for k in range(LEVELS):
        one = total[:, 32 * k : 32 * k + 32]
        row = jnp.where(mine, rhs_ref[:, 128 * k : 128 * k + 128] - jnp.concatenate([one] * 4, 1), 0.0)
        pend_ref[k] = row
        if k == 0:
            first = row
    turned = block_swap(first)
    chunk = turned[0:4] + turned[4:8] + turned[8:12] + turned[12:16]
    msg_ref[...] = jnp.concatenate([chunk] * 32, 0)


def run_own_start(place, got, rhs, after):
    return call(
        own_start,
        (sds((LEVELS, V, 128)), sds((128, 128)), sds((128, 128))),
        [SMEM, VM, VM, ANY],
        (VM, VM, VM),
        flops=1 << 27,
        nbytes=1 << 19,
    )(place, got, rhs, after)


def columns_of(got_ref, parts):
    total = got_ref[pl.ds(0, 128), :]
    for p in range(1, parts):
        total += got_ref[pl.ds(128 * p, 128), :]
    return jnp.concatenate([block_swap(total[16 * t : 16 * t + 16]) for t in range(8)], 1)


def row_message(msg_ref, rows):
    turned = block_swap(rows)
    for q in range(4):
        msg_ref[pl.ds(128 * q, 128), :] = jnp.concatenate([turned[4 * q : 4 * q + 4]] * 32, 0)


def block_parts(block):
    return jnp.concatenate(split(block.reshape(ROWS, COLS)), 0)


def times_columns(x, w):
    out = dot(jnp.concatenate(split(x), 0), w, NT)
    return (out[:V, :ROWS] + out[V:, :ROWS]) + (out[:V, ROWS:] + out[V:, ROWS:])


def times_rows(x, w):
    half = jnp.concatenate(split(x), 0)
    out = dot(jnp.concatenate([half, half], 1), w, NN)
    return out[:V] + out[V:]


PARTS = (2 * ROWS, COLS)


def buffers(count):
    return [pltpu.VMEM((count, 4, 32, COLS), F32), pltpu.SemaphoreType.DMA((count,))]


def block_of(panels_ref, diag_ref, upper, lower):
    return diag_ref.at[lower, :, 0] if upper == lower else panels_ref.at[pair_index(upper, lower), :, 0]


def first_block(after_ref, panels_ref, w_ref, buffer, sems):
    fetch([panels_ref.at[pair_index(1, 0), :, 0]], buffer, sems)[0].wait()
    w_ref[...] = block_parts(buffer[0])


def run_first_block(after, panels):
    return call(first_block, sds(PARTS, BF16), [ANY, HBM], VM, scratch=buffers(1), flops=1 << 20, nbytes=1 << 20)(
        after, panels
    )


def forward_step(level, parts, count, *refs):
    got_ref, pend_ref = refs[:2]
    earlier, blocks, (x_ref, msg_ref) = refs[2 : 1 + count], refs[1 + count : 1 + 2 * count], refs[-2:]
    x = columns_of(got_ref, parts)
    x_ref[...] = x
    rows = pend_ref[level]
    for one, w_ref in zip([r[...] for r in earlier] + [x], blocks):
        rows -= times_columns(one, w_ref[...])
    row_message(msg_ref, rows)


def run_forward_step(level, parts, got, pend, earlier, blocks):
    return call(
        functools.partial(forward_step, level, parts, len(blocks)),
        (sds((V, COLS)), sds((512, 128))),
        [VM] * (2 + len(earlier) + len(blocks)),
        (VM, VM),
        flops=len(blocks) << 24,
        nbytes=len(blocks) << 20,
    )(got, pend, *earlier, *blocks)


def forward_rest(levels, wanted, *refs):
    n = len(levels)
    x_refs, (pend_ref, panels_ref, diag_ref), refs = refs[:n], refs[n : n + 3], refs[n + 3 :]
    out_ref, y_refs, w_refs, (buffer, sems) = refs[0], refs[1 : 1 + n], refs[1 + n : -2], refs[-2:]
    later = range(levels[-1] + 2, LEVELS)
    pairs = [(j, k) for j in later for k in levels] + [(k, k) for k in levels] + list(wanted)
    copies = fetch([block_of(panels_ref, diag_ref, *pair) for pair in pairs], buffer, sems)
    out_ref[...] = pend_ref[...]
    slot = 0
    for j in later:
        rows = pend_ref[j]
        for x_ref in x_refs:
            copies[slot].wait()
            rows -= times_columns(x_ref[...], block_parts(buffer[slot]))
            slot += 1
        out_ref[j] = rows
    for x_ref, y_ref in zip(x_refs, y_refs):
        copies[slot].wait()
        y_ref[...] = times_columns(x_ref[...], block_parts(buffer[slot]))
        slot += 1
    for w_ref in w_refs:
        copies[slot].wait()
        w_ref[...] = block_parts(buffer[slot])
        slot += 1


def run_forward_rest(levels, xs, pend, panels, diag, wanted):
    n = len(levels)
    count = n * (LEVELS - 1 - levels[-1]) + len(wanted)
    out = call(
        functools.partial(forward_rest, levels, wanted),
        (sds((LEVELS, V, 128)), *[sds((V, 128))] * n, *[sds(PARTS, BF16)] * len(wanted)),
        [VM] * n + [VM, HBM, HBM],
        (VM,) * (1 + n + len(wanted)),
        scratch=buffers(count),
        flops=count << 24,
        nbytes=count << 19,
    )(*xs, pend, panels, diag)
    return out[0], out[1 : 1 + n], out[1 + n :]


def forward_last(got_ref, y0, y1, y2, y3, y4, w_ref, msg_ref):
    x = columns_of(got_ref, 4)
    last = times_columns(x, w_ref[...])
    for l in range(4):
        for k, one in enumerate((y0, y1, y2, y3, y4)):
            msg_ref[pl.ds(96 * l + 16 * k, 16), :] = one[...]
        msg_ref[pl.ds(96 * l + 80, 16), :] = last


def run_forward_last(got, ys, w):
    return call(
        forward_last,
        sds((4 * 96, 128)),
        [VM] + [VM] * 5 + [VM],
        VM,
        flops=1 << 24,
        nbytes=1 << 20,
    )(got, *ys, w)


def column_message(msg_ref, columns):
    for t in range(8):
        turned = block_swap(columns[:, 128 * t : 128 * t + 128])
        for l in range(4):
            msg_ref[pl.ds(128 * l + 16 * t, 16), :] = turned


def backward_start(got_ref, w_ref, y_ref, msg_ref):
    y = got_ref[pl.ds(0, 96), :]
    for l in range(1, 4):
        y += got_ref[pl.ds(96 * l, 96), :]
    y_ref[...] = y
    column_message(msg_ref, times_rows(y[80:96], w_ref[...]))


def run_backward_start(got, w):
    return call(
        backward_start,
        (sds((96, 128)), sds((512, 128))),
        [VM, VM],
        (VM, VM),
        flops=1 << 24,
        nbytes=1 << 20,
    )(got, w)


def backward_diag(wanted, y_ref, panels_ref, diag_ref, out_ref, *refs):
    w_refs, (buffer, sems) = refs[:-2], refs[-2:]
    count = LEVELS - 1
    pairs = [(k, k) for k in range(count)] + list(wanted)
    copies = fetch([block_of(panels_ref, diag_ref, *pair) for pair in pairs], buffer, sems)
    for k in range(count):
        copies[k].wait()
        out_ref[k] = times_rows(y_ref[pl.ds(16 * k, 16), :], block_parts(buffer[k]))
    for n, w_ref in enumerate(w_refs):
        copies[count + n].wait()
        w_ref[...] = block_parts(buffer[count + n])


def run_backward_diag(y, panels, diag, wanted):
    out = call(
        functools.partial(backward_diag, wanted),
        (sds((LEVELS - 1, V, COLS)), *[sds(PARTS, BF16)] * len(wanted)),
        [VM, HBM, HBM],
        (VM,) * (1 + len(wanted)),
        scratch=buffers(LEVELS - 1 + len(wanted)),
        flops=8 << 24,
        nbytes=4 << 20,
    )(y, panels, diag)
    return out[0], out[1:]


def rows_of(got_ref):
    parts = []
    for q in range(4):
        total = got_ref[pl.ds(128 * q, 8), :]
        for t in range(1, 16):
            total += got_ref[pl.ds(128 * q + 8 * t, 8), :]
        parts.append(total[0:4] + total[4:8])
    return block_swap(jnp.concatenate(parts, 0))


def backward_step(level, count, *refs):
    got_ref, pend_ref = refs[:2]
    earlier, blocks, (x_ref, msg_ref) = refs[2 : 1 + count], refs[1 + count : 1 + 2 * count], refs[-2:]
    x = rows_of(got_ref)
    x_ref[...] = x
    columns = pend_ref[level]
    for one, w_ref in zip([r[...] for r in earlier] + [x], blocks):
        columns -= times_rows(one, w_ref[...])
    column_message(msg_ref, columns)


def run_backward_step(level, got, pend, earlier, blocks):
    return call(
        functools.partial(backward_step, level, len(blocks)),
        (sds((V, 128)), sds((512, 128))),
        [VM] * (2 + len(earlier) + len(blocks)),
        (VM, VM),
        flops=len(blocks) << 24,
        nbytes=len(blocks) << 20,
    )(got, pend, *earlier, *blocks)


def backward_rest(levels, wanted, *refs):
    n = len(levels)
    x_refs, (pend_ref, panels_ref), refs = refs[:n], refs[n : n + 2], refs[n + 2 :]
    out_ref, w_refs, (buffer, sems) = refs[0], refs[1:-2], refs[-2:]
    lower = range(levels[-1] - 2, -1, -1)
    pairs = [(k, j) for j in lower for k in levels] + list(wanted)
    copies = fetch([block_of(panels_ref, None, *pair) for pair in pairs], buffer, sems)
    slot = 0
    for j in lower:
        columns = pend_ref[j]
        for x_ref in x_refs:
            copies[slot].wait()
            columns -= times_rows(x_ref[...], block_parts(buffer[slot]))
            slot += 1
        out_ref[j] = columns
    for w_ref in w_refs:
        copies[slot].wait()
        w_ref[...] = block_parts(buffer[slot])
        slot += 1


def run_backward_rest(levels, xs, pend, panels, wanted):
    n, lower = len(levels), levels[-1] - 1
    count = n * lower + len(wanted)
    out = call(
        functools.partial(backward_rest, levels, wanted),
        (sds((lower, V, COLS)), *[sds(PARTS, BF16)] * len(wanted)),
        [VM] * n + [VM, HBM],
        (VM,) * (1 + len(wanted)),
        scratch=buffers(count),
        flops=count << 24,
        nbytes=count << 19,
    )(*xs, pend, panels)
    return out[0], out[1:]


def own_finish(place_ref, got_ref, x1, x2, x3, x4, x5, index_ref, x_ref, msg_ref):
    x0 = rows_of(got_ref)
    levels = [x0] + [r[...] for r in (x1, x2, x3, x4, x5)]
    mine = []
    for k, x in enumerate(levels):
        one = jnp.zeros((V, 32), F32)
        for q in range(4):
            x_ref[pl.ds(4 * k + q, V, 4 * LEVELS), :] = x[:, 32 * q : 32 * q + 32]
            one = jnp.where(place_ref[0] == q, x[:, 32 * q : 32 * q + 32], one)
        mine.append(one)
    rows = jnp.concatenate(mine + [jnp.zeros((V, 64), F32)], 1)
    high, low = split(jnp.concatenate([rows] * 8, 0))
    table = jnp.concatenate([high, low], 0)
    index = index_ref[...]
    column = (iota((128, 256), 1) + 1).astype(F32)
    group = iota((128, 128), 1) >> 4
    for half in range(2):
        out = jnp.zeros((128, 128), F32)
        for g in range(8):
            j = 8 * half + g
            hot = jnp.where(index[:, j : j + 1] == column, 1.0, 0.0).astype(BF16)
            got = dot(hot, table, NT)
            out = jnp.where(group == g, got[:, :128] + got[:, 128:], out)
        msg_ref[pl.ds(half, 128, 2), :] = out


def run_own_finish(place, got, xs, index):
    return call(
        own_finish,
        (sds((V * LEVELS * 4, 32)), sds((256, 128))),
        [SMEM, VM] + [VM] * 5 + [VM],
        (VM, VM),
        flops=1 << 27,
        nbytes=1 << 20,
    )(place, got, *xs, index)


def exchange(message, axis=ALL):
    return lax.all_to_all(message, axis, 0, 0, tiled=True)


def per_device(leaf_rhs, leaf_inv, update_blocks, row_map, live_rows, sep_rhs, inv_diag, panels):
    place = lax.axis_index("leaf").astype(jnp.int32).reshape(1)
    rhs = sep_rhs.reshape(V, LEVELS * 128)
    leaf_y, message, table, rank = run_leaf_forward(live_rows, leaf_rhs, row_map, leaf_inv, update_blocks)
    got = exchange(message)
    block = run_first_block(leaf_y, panels)
    pend, message, index = run_own_start(place, got, rhs, block)
    got = exchange(message, "sep")
    x0, message = run_forward_step(1, 1, got, pend, [], [block])
    got = exchange(message)
    pend, (y0,), (near, far, last) = run_forward_rest((0,), [x0], pend, panels, inv_diag, ((2, 1), (3, 1), (3, 2)))
    x1, message = run_forward_step(2, 4, got, pend, [], [near])
    x2, message = run_forward_step(3, 4, exchange(message), pend, [x1], [far, last])
    got = exchange(message)
    pend, (y1, y2), (near, far, last) = run_forward_rest(
        (1, 2), [x1, x2], pend, panels, inv_diag, ((4, 3), (5, 3), (5, 4))
    )
    x3, message = run_forward_step(4, 4, got, pend, [], [near])
    x4, message = run_forward_step(5, 4, exchange(message), pend, [x3], [far, last])
    got = exchange(message)
    _, (y3, y4), (block,) = run_forward_rest((3, 4), [x3, x4], pend, panels, inv_diag, ((5, 5),))
    message = run_forward_last(got, [y0, y1, y2, y3, y4], block)
    y, message = run_backward_start(exchange(message, "leaf"), block)
    got = exchange(message)
    pend, (near, far, last) = run_backward_diag(y, panels, inv_diag, ((5, 4), (5, 3), (4, 3)))
    s5, message = run_backward_step(4, got, pend, [], [near])
    s4, message = run_backward_step(3, exchange(message), pend, [s5], [far, last])
    got = exchange(message)
    pend, (near, far, last) = run_backward_rest((5, 4), [s5, s4], pend, panels, ((3, 2), (3, 1), (2, 1)))
    s3, message = run_backward_step(2, got, pend, [], [near])
    s2, message = run_backward_step(1, exchange(message), pend, [s3], [far, last])
    got = exchange(message)
    pend, (block,) = run_backward_rest((3, 2), [s3, s2], pend, panels, ((1, 0),))
    s1, message = run_backward_step(0, got, pend, [], [block])
    got = exchange(message)
    xs = [s1, s2, s3, s4, s5]
    rows, message = run_own_finish(place, got, xs, index)
    got = exchange(message)
    leaf_x = run_leaf_backward(live_rows, got, table, rank, leaf_y, leaf_inv, update_blocks)
    sep_solution = rows.reshape(V, LEVELS, 4, 1, 32)
    return leaf_x, sep_solution


def solution(mesh):
    in_specs = (
        P(ALL, None, None),
        P(ALL, None, None),
        P(ALL, None, None),
        P(ALL, None),
        P(ALL),
        P(None, None, None, "sep", None),
        P(None, None, "sep", None, "leaf"),
        P(None, None, "sep", None, "leaf"),
    )
    out_specs = (P(ALL, None, None), P(None, None, None, "sep", None))
    return jax.shard_map(per_device, mesh=mesh, in_specs=in_specs, out_specs=out_specs, check_vma=False)
```

```python
import functools

import jax
import jax.numpy as jnp
from jax import lax
from jax.experimental import pallas as pl
from jax.experimental.pallas import tpu as pltpu
from jax.sharding import PartitionSpec as P

F32 = jnp.float32
BF16 = jnp.bfloat16
V = 16
LEVELS = 6
ROWS = 128
COLS = 1024
UPD = 1024
CHUNKS = 2
ALL = ("leaf", "sep")
VMEM_LIMIT = 51 * 1024 * 1024
NT = (((1,), (1,)), ((), ()))
NN = (((1,), (0,)), ((), ()))


def pair_index(upper, lower):
    return lower * (LEVELS - 1) - lower * (lower - 1) // 2 + upper - lower - 1


def iota(shape, dim):
    return lax.broadcasted_iota(jnp.int32, shape, dim)


def dot(a, b, dims):
    return lax.dot_general(a, b, dims, preferred_element_type=F32)


def split(x):
    high = x.astype(BF16)
    return high, (x - high.astype(F32)).astype(BF16)


def product(x, w, dims):
    xh, xl = split(x)
    wh, wl = split(w)
    m = x.shape[0]
    both = dot(jnp.concatenate([xh, xl], 0), wh, dims)
    return both[:m] + both[m:] + dot(xh, wl, dims)


def exact_rows(x, onehot, dims):
    xh, xl = split(x)
    m = x.shape[0]
    both = dot(jnp.concatenate([xh, xl], 0), onehot, dims)
    return both[:m] + both[m:]


def block_swap(t):
    gap = (iota((16, 128), 1) // 32 - iota((16, 128), 0) // 4) & 3
    out = t
    for d in range(1, 4):
        moved = pltpu.roll(pltpu.roll(t, 32 * d, 1), 16 - 4 * d, 0)
        out = jnp.where(gap == d, moved, out)
    return out


def call(body, out_shape, in_specs, out_specs, scratch=(), flops=0, nbytes=0, limit=VMEM_LIMIT):
    return pl.pallas_call(
        body,
        out_shape=out_shape,
        in_specs=in_specs,
        out_specs=out_specs,
        scratch_shapes=scratch,
        compiler_params=pltpu.CompilerParams(vmem_limit_bytes=limit),
        cost_estimate=pl.CostEstimate(flops=flops, bytes_accessed=nbytes, transcendentals=0),
    )


def sds(shape, dtype=F32):
    return jax.ShapeDtypeStruct(shape, dtype)


VM = pl.BlockSpec(memory_space=pltpu.VMEM)
SMEM = pl.BlockSpec(memory_space=pltpu.SMEM)
ANY = pl.BlockSpec(memory_space=pl.ANY)
HBM = pl.BlockSpec(memory_space=pltpu.HBM)


def fetch(sources, buffer, sems):
    copies = [pltpu.make_async_copy(src, buffer.at[n], sems.at[n]) for n, src in enumerate(sources)]
    for one in copies:
        one.start()
    return copies


def leaf_forward(live_ref, rhs_hbm, map_hbm, inv_ref, upd_ref, y_ref, msg_ref, t_ref, rank_ref, rhs_ref, map_ref, buffer, sems):
    step = UPD // CHUNKS
    small = [pltpu.make_async_copy(map_hbm, map_ref, sems.at[2 * CHUNKS]), pltpu.make_async_copy(rhs_hbm, rhs_ref, sems.at[2 * CHUNKS + 1])]
    for one in small:
        one.start()
    sources = []
    for n in range(CHUNKS):
        for ref in (inv_ref, upd_ref):
            sources.append(ref.at[0, pl.ds(step * n, step), :])
    copies = fetch(sources, buffer, sems)
    small[0].wait()
    rows = map_ref[...]
    owner = (rows >> 5) & 127
    hot = (iota((128, UPD), 0) == owner).astype(F32)
    ones = jnp.where((iota((128, 256), 0) < iota((128, 256), 1)), 1.0, 0.0).astype(BF16)
    carry = jnp.zeros((128, 128), F32)
    before = []
    for n in range(UPD // 128):
        counts = dot(hot[:, 128 * n : 128 * n + 128].astype(BF16), ones, NN)
        before.append(counts[:, :128] + carry)
        carry += counts[:, 128:]
    before = jnp.concatenate(before, 1)
    rank = jnp.sum(hot * before, axis=0, keepdims=True).astype(jnp.int32)
    rank_ref[...] = jnp.broadcast_to(rank, rank_ref.shape)
    for half in range(2):
        t_ref[pl.ds(128 * half, 128), :] = jnp.where((rank >> 3) == half, hot, 0.0).astype(BF16)
    live = iota((1, UPD), 1) < live_ref[0]
    local = (rows >> 12) * 32 + (rows & 31) + 1
    places = jnp.where((iota((128, UPD), 0) == rank) & live, local.astype(F32), 0.0)
    msg_ref[pl.ds(2, 128, 4), :] = dot(hot.astype(BF16), places.astype(BF16), NT)
    msg_ref[pl.ds(3, 128, 4), :] = jnp.zeros((128, 128), F32)
    acc = jnp.zeros((V, UPD), F32)
    small[1].wait()
    for n in range(CHUNKS):
        copies[2 * n].wait()
        y_part = product(rhs_ref[0], buffer[2 * n], NT)
        y_ref[:, step * n : step * n + step] = y_part
        copies[2 * n + 1].wait()
        acc += product(y_part, buffer[2 * n + 1], NN)
    group = iota((128, UPD), 0) >> 4
    spread = jnp.where((group == (rank & 7)) & live, jnp.concatenate([acc] * 8, 0), 0.0)
    parts = jnp.concatenate(split(spread), 0)
    for half in range(2):
        got = dot(t_ref[pl.ds(128 * half, 128), :], parts, NT)
        msg_ref[pl.ds(half, 128, 4), :] = got[:, :128] + got[:, 128:]


def run_leaf_forward(live, rhs, rows, inv, upd):
    return call(
        leaf_forward,
        (sds((V, UPD)), sds((512, 128)), sds((256, UPD), BF16), sds((8, UPD), jnp.int32)),
        [SMEM, HBM, HBM, HBM, HBM],
        (VM, VM, VM, VM),
        scratch=[
            pltpu.VMEM((1, V, 1024), F32),
            pltpu.VMEM((1, UPD), jnp.int32),
            pltpu.VMEM((2 * CHUNKS, UPD // CHUNKS, 1024), F32),
            pltpu.SemaphoreType.DMA((2 * CHUNKS + 2,)),
        ],
        flops=2 * 16 * 3 * (2 << 20),
        nbytes=8 << 20,
        limit=60 * 1024 * 1024,
    )(live, rhs, rows, inv, upd)


def leaf_backward(live_ref, got_ref, t_ref, rank_ref, y_ref, inv_ref, upd_ref, out_ref, buffer, sems):
    step = UPD // CHUNKS
    sources = []
    for n in range(CHUNKS):
        for ref in (upd_ref, inv_ref):
            sources.append(ref.at[0, pl.ds(step * n, step), :])
    copies = fetch(sources, buffer, sems)
    live = iota((1, UPD), 1) < live_ref[0]
    group = iota((128, UPD), 0) >> 4
    total = jnp.zeros((128, UPD), F32)
    for half in range(2):
        values = got_ref[pl.ds(half, 128, 2), :].T
        total += exact_rows(values, t_ref[pl.ds(128 * half, 128), :], NN)
    total = jnp.where((group == (rank_ref[0:1, :] & 7)) & live, total, 0.0)
    mapped = total[0:16]
    for g in range(1, 8):
        mapped += total[16 * g : 16 * g + 16]
    out = jnp.zeros((V, 1024), F32)
    for n in range(CHUNKS):
        copies[2 * n].wait()
        z = y_ref[:, step * n : step * n + step] - product(mapped, buffer[2 * n], NT)
        copies[2 * n + 1].wait()
        out += product(z, buffer[2 * n + 1], NN)
    out_ref[0] = out


def run_leaf_backward(live, got, t, rank, y, inv, upd):
    return call(
        leaf_backward,
        sds((1, V, 1024)),
        [SMEM, VM, VM, VM, VM, HBM, HBM],
        VM,
        scratch=[pltpu.VMEM((2 * CHUNKS, UPD // CHUNKS, 1024), F32), pltpu.SemaphoreType.DMA((2 * CHUNKS,))],
        flops=2 * 16 * 3 * (2 << 20),
        nbytes=8 << 20,
    )(live, got, t, rank, y, inv, upd)


def own_start(place_ref, got_ref, rhs_ref, after_ref, pend_ref, msg_ref, index_ref):
    values = [got_ref[pl.ds(half, 128, 4), :].T for half in range(2)]
    index = got_ref[pl.ds(2, 128, 4), :]
    index_ref[...] = index
    column = (iota((128, 256), 1) + 1).astype(F32)
    hot, rows = [], []
    for half in range(2):
        for g in range(8):
            j = 8 * half + g
            hot.append(jnp.where(index[:, j : j + 1] == column, 1.0, 0.0).astype(BF16))
            rows.append(values[half][16 * g : 16 * g + 16])
    total = exact_rows(jnp.concatenate(rows, 1), jnp.concatenate(hot, 0), NN)
    mine = iota((V, 128), 1) // 32 == place_ref[0]
    first = None
    for k in range(LEVELS):
        one = total[:, 32 * k : 32 * k + 32]
        row = jnp.where(mine, rhs_ref[:, 128 * k : 128 * k + 128] - jnp.concatenate([one] * 4, 1), 0.0)
        pend_ref[k] = row
        if k == 0:
            first = row
    turned = block_swap(first)
    chunk = turned[0:4] + turned[4:8] + turned[8:12] + turned[12:16]
    msg_ref[...] = jnp.concatenate([chunk] * 32, 0)


def run_own_start(place, got, rhs, after):
    return call(
        own_start,
        (sds((LEVELS, V, 128)), sds((128, 128)), sds((128, 128))),
        [SMEM, VM, VM, ANY],
        (VM, VM, VM),
        flops=1 << 27,
        nbytes=1 << 19,
    )(place, got, rhs, after)


def columns_of(got_ref, parts):
    total = got_ref[pl.ds(0, 128), :]
    for p in range(1, parts):
        total += got_ref[pl.ds(128 * p, 128), :]
    return jnp.concatenate([block_swap(total[16 * t : 16 * t + 16]) for t in range(8)], 1)


def row_message(msg_ref, rows):
    turned = block_swap(rows)
    for q in range(4):
        msg_ref[pl.ds(128 * q, 128), :] = jnp.concatenate([turned[4 * q : 4 * q + 4]] * 32, 0)


def block_parts(block):
    return jnp.concatenate(split(block.reshape(ROWS, COLS)), 0)


def times_columns(x, w):
    out = dot(jnp.concatenate(split(x), 0), w, NT)
    return (out[:V, :ROWS] + out[V:, :ROWS]) + (out[:V, ROWS:] + out[V:, ROWS:])


def times_rows(x, w):
    half = jnp.concatenate(split(x), 0)
    out = dot(jnp.concatenate([half, half], 1), w, NN)
    return out[:V] + out[V:]


PARTS = (2 * ROWS, COLS)


def buffers(count):
    return [pltpu.VMEM((count, 4, 32, COLS), F32), pltpu.SemaphoreType.DMA((count,))]


def block_of(panels_ref, diag_ref, upper, lower):
    return diag_ref.at[lower, :, 0] if upper == lower else panels_ref.at[pair_index(upper, lower), :, 0]


FIRST = ((1, 0), (2, 0), (2, 1))


def first_blocks(after_ref, panels_ref, *refs):
    w_refs, (buffer, sems) = refs[:-2], refs[-2:]
    copies = fetch([block_of(panels_ref, None, *pair) for pair in FIRST], buffer, sems)
    for n, w_ref in enumerate(w_refs):
        copies[n].wait()
        w_ref[...] = block_parts(buffer[n])


def run_first_blocks(after, panels):
    n = len(FIRST)
    return call(
        first_blocks,
        [sds(PARTS, BF16)] * n,
        [ANY, HBM],
        [VM] * n,
        scratch=buffers(n),
        flops=n << 20,
        nbytes=n << 20,
    )(after, panels)


def forward_step(level, parts, count, *refs):
    got_ref, pend_ref = refs[:2]
    earlier, blocks, (x_ref, msg_ref) = refs[2 : 1 + count], refs[1 + count : 1 + 2 * count], refs[-2:]
    x = columns_of(got_ref, parts)
    x_ref[...] = x
    rows = pend_ref[level]
    for one, w_ref in zip([r[...] for r in earlier] + [x], blocks):
        rows -= times_columns(one, w_ref[...])
    row_message(msg_ref, rows)


def run_forward_step(level, parts, got, pend, earlier, blocks):
    return call(
        functools.partial(forward_step, level, parts, len(blocks)),
        (sds((V, COLS)), sds((512, 128))),
        [VM] * (2 + len(earlier) + len(blocks)),
        (VM, VM),
        flops=len(blocks) << 24,
        nbytes=len(blocks) << 20,
    )(got, pend, *earlier, *blocks)


def forward_rest(levels, wanted, *refs):
    n = len(levels)
    x_refs, (pend_ref, panels_ref, diag_ref), refs = refs[:n], refs[n : n + 3], refs[n + 3 :]
    out_ref, y_refs, w_refs, (buffer, sems) = refs[0], refs[1 : 1 + n], refs[1 + n : -2], refs[-2:]
    later = range(levels[-1] + 2, LEVELS)
    pairs = [(j, k) for j in later for k in levels] + [(k, k) for k in levels] + list(wanted)
    copies = fetch([block_of(panels_ref, diag_ref, *pair) for pair in pairs], buffer, sems)
    out_ref[...] = pend_ref[...]
    slot = 0
    for j in later:
        rows = pend_ref[j]
        for x_ref in x_refs:
            copies[slot].wait()
            rows -= times_columns(x_ref[...], block_parts(buffer[slot]))
            slot += 1
        out_ref[j] = rows
    for x_ref, y_ref in zip(x_refs, y_refs):
        copies[slot].wait()
        y_ref[...] = times_columns(x_ref[...], block_parts(buffer[slot]))
        slot += 1
    for w_ref in w_refs:
        copies[slot].wait()
        w_ref[...] = block_parts(buffer[slot])
        slot += 1


def run_forward_rest(levels, xs, pend, panels, diag, wanted):
    n = len(levels)
    count = n * (LEVELS - 1 - levels[-1]) + len(wanted)
    out = call(
        functools.partial(forward_rest, levels, wanted),
        (sds((LEVELS, V, 128)), *[sds((V, 128))] * n, *[sds(PARTS, BF16)] * len(wanted)),
        [VM] * n + [VM, HBM, HBM],
        (VM,) * (1 + n + len(wanted)),
        scratch=buffers(count),
        flops=count << 24,
        nbytes=count << 19,
    )(*xs, pend, panels, diag)
    return out[0], out[1 : 1 + n], out[1 + n :]


def forward_last(got_ref, y0, y1, y2, y3, x4_ref, w4_ref, w5_ref, msg_ref):
    y4 = times_columns(x4_ref[...], w4_ref[...])
    y5 = times_columns(columns_of(got_ref, 4), w5_ref[...])
    for l in range(4):
        for k, one in enumerate((y0, y1, y2, y3)):
            msg_ref[pl.ds(96 * l + 16 * k, 16), :] = one[...]
        msg_ref[pl.ds(96 * l + 64, 16), :] = y4
        msg_ref[pl.ds(96 * l + 80, 16), :] = y5


def run_forward_last(got, ys, x4, w4, w5):
    return call(
        forward_last,
        sds((4 * 96, 128)),
        [VM] * 8,
        VM,
        flops=2 << 24,
        nbytes=1 << 20,
    )(got, *ys, x4, w4, w5)


def column_message(msg_ref, columns):
    for t in range(8):
        turned = block_swap(columns[:, 128 * t : 128 * t + 128])
        for l in range(4):
            msg_ref[pl.ds(128 * l + 16 * t, 16), :] = turned


def backward_start(got_ref, w_ref, y_ref, msg_ref):
    y = got_ref[pl.ds(0, 96), :]
    for l in range(1, 4):
        y += got_ref[pl.ds(96 * l, 96), :]
    y_ref[...] = y
    column_message(msg_ref, times_rows(y[80:96], w_ref[...]))


def run_backward_start(got, w):
    return call(
        backward_start,
        (sds((96, 128)), sds((512, 128))),
        [VM, VM],
        (VM, VM),
        flops=1 << 24,
        nbytes=1 << 20,
    )(got, w)


def rows_of(got_ref):
    parts = []
    for q in range(4):
        total = got_ref[pl.ds(128 * q, 8), :]
        for t in range(1, 16):
            total += got_ref[pl.ds(128 * q + 8 * t, 8), :]
        parts.append(total[0:4] + total[4:8])
    return block_swap(jnp.concatenate(parts, 0))


def backward_step(level, count, *refs):
    got_ref, pend_ref = refs[:2]
    earlier, blocks, (x_ref, msg_ref) = refs[2 : 1 + count], refs[1 + count : 1 + 2 * count], refs[-2:]
    x = rows_of(got_ref)
    x_ref[...] = x
    columns = pend_ref[level]
    for one, w_ref in zip([r[...] for r in earlier] + [x], blocks):
        columns -= times_rows(one, w_ref[...])
    column_message(msg_ref, columns)


def run_backward_step(level, got, pend, earlier, blocks):
    return call(
        functools.partial(backward_step, level, len(blocks)),
        (sds((V, 128)), sds((512, 128))),
        [VM] * (2 + len(earlier) + len(blocks)),
        (VM, VM),
        flops=len(blocks) << 24,
        nbytes=len(blocks) << 20,
    )(got, pend, *earlier, *blocks)


def backward_next(got_ref, y_ref, diag_ref, w_ref, x_ref, msg_ref):
    x = rows_of(got_ref)
    x_ref[...] = x
    column_message(msg_ref, times_rows(y_ref[64:80, :], diag_ref[...]) - times_rows(x, w_ref[...]))


def run_backward_next(got, y, diag, w):
    return call(
        backward_next,
        (sds((V, 128)), sds((512, 128))),
        [VM] * 4,
        (VM, VM),
        flops=2 << 24,
        nbytes=1 << 20,
    )(got, y, diag, w)


def backward_diag(wanted, y_ref, x_ref, panels_ref, diag_ref, out_ref, *refs):
    w_refs, (buffer, sems) = refs[:-2], refs[-2:]
    pairs = [(up, k) for k in range(LEVELS - 2) for up in (k, LEVELS - 1)] + list(wanted)
    copies = fetch([block_of(panels_ref, diag_ref, *pair) for pair in pairs], buffer, sems)
    for k in range(LEVELS - 2):
        copies[2 * k].wait()
        columns = times_rows(y_ref[pl.ds(16 * k, 16), :], block_parts(buffer[2 * k]))
        copies[2 * k + 1].wait()
        out_ref[k] = columns - times_rows(x_ref[...], block_parts(buffer[2 * k + 1]))
    for n, w_ref in enumerate(w_refs):
        slot = 2 * (LEVELS - 2) + n
        copies[slot].wait()
        w_ref[...] = block_parts(buffer[slot])


def run_backward_diag(y, x, panels, diag, wanted):
    out = call(
        functools.partial(backward_diag, wanted),
        (sds((LEVELS - 2, V, COLS)), *[sds(PARTS, BF16)] * len(wanted)),
        [VM, VM, HBM, HBM],
        (VM,) * (1 + len(wanted)),
        scratch=buffers(2 * (LEVELS - 2) + len(wanted)),
        flops=11 << 24,
        nbytes=6 << 20,
    )(y, x, panels, diag)
    return out[0], out[1:]


def backward_rest(levels, wanted, *refs):
    n = len(levels)
    x_refs, (pend_ref, panels_ref), refs = refs[:n], refs[n : n + 2], refs[n + 2 :]
    out_ref, w_refs, (buffer, sems) = refs[0], refs[1:-2], refs[-2:]
    lower = range(levels[-1] - 2, -1, -1)
    pairs = [(k, j) for j in lower for k in levels] + list(wanted)
    copies = fetch([block_of(panels_ref, None, *pair) for pair in pairs], buffer, sems)
    slot = 0
    for j in lower:
        columns = pend_ref[j]
        for x_ref in x_refs:
            copies[slot].wait()
            columns -= times_rows(x_ref[...], block_parts(buffer[slot]))
            slot += 1
        out_ref[j] = columns
    for w_ref in w_refs:
        copies[slot].wait()
        w_ref[...] = block_parts(buffer[slot])
        slot += 1


def run_backward_rest(levels, xs, pend, panels, wanted):
    n, lower = len(levels), levels[-1] - 1
    count = n * lower + len(wanted)
    out = call(
        functools.partial(backward_rest, levels, wanted),
        (sds((lower, V, COLS)), *[sds(PARTS, BF16)] * len(wanted)),
        [VM] * n + [VM, HBM],
        (VM,) * (1 + len(wanted)),
        scratch=buffers(count),
        flops=count << 24,
        nbytes=count << 19,
    )(*xs, pend, panels)
    return out[0], out[1:]


def own_finish(place_ref, got_ref, x1, x2, x3, x4, x5, index_ref, x_ref, msg_ref):
    x0 = rows_of(got_ref)
    levels = [x0] + [r[...] for r in (x1, x2, x3, x4, x5)]
    mine = []
    for k, x in enumerate(levels):
        one = jnp.zeros((V, 32), F32)
        for q in range(4):
            x_ref[pl.ds(4 * k + q, V, 4 * LEVELS), :] = x[:, 32 * q : 32 * q + 32]
            one = jnp.where(place_ref[0] == q, x[:, 32 * q : 32 * q + 32], one)
        mine.append(one)
    rows = jnp.concatenate(mine + [jnp.zeros((V, 64), F32)], 1)
    high, low = split(jnp.concatenate([rows] * 8, 0))
    table = jnp.concatenate([high, low], 0).astype(F32)
    index = index_ref[...]
    column = (iota((128, 256), 1) + 1).astype(F32)
    group = (iota((256, 256), 0) >> 4) & 7
    hot, tables = [], []
    for g in range(8):
        pair = [jnp.where(index[:, j : j + 1] == column, 1.0, 0.0) for j in (g, 8 + g)]
        hot.append(jnp.concatenate(pair, 0).astype(BF16))
        tables.append(jnp.where(group == g, table, 0.0).astype(BF16))
    got = dot(jnp.concatenate(hot, 1), jnp.concatenate(tables, 1), NT)
    for half in range(2):
        part = got[128 * half : 128 * half + 128]
        msg_ref[pl.ds(half, 128, 2), :] = part[:, :128] + part[:, 128:]


def run_own_finish(place, got, xs, index):
    return call(
        own_finish,
        (sds((V * LEVELS * 4, 32)), sds((256, 128))),
        [SMEM, VM] + [VM] * 5 + [VM],
        (VM, VM),
        flops=1 << 27,
        nbytes=1 << 20,
    )(place, got, *xs, index)


def exchange(message, axis=ALL):
    return lax.all_to_all(message, axis, 0, 0, tiled=True)


def per_device(leaf_rhs, leaf_inv, update_blocks, row_map, live_rows, sep_rhs, inv_diag, panels):
    place = lax.axis_index("leaf").astype(jnp.int32).reshape(1)
    rhs = sep_rhs.reshape(V, LEVELS * 128)
    leaf_y, message, table, rank = run_leaf_forward(live_rows, leaf_rhs, row_map, leaf_inv, update_blocks)
    got = exchange(message)
    first, far, near = run_first_blocks(leaf_y, panels)
    pend, message, index = run_own_start(place, got, rhs, near)
    got = exchange(message, "sep")
    x0, message = run_forward_step(1, 1, got, pend, [], [first])
    x1, message = run_forward_step(2, 4, exchange(message), pend, [x0], [far, near])
    got = exchange(message)
    pend, (y0, y1), (first, far, near) = run_forward_rest(
        (0, 1), [x0, x1], pend, panels, inv_diag, ((3, 2), (4, 2), (4, 3))
    )
    x2, message = run_forward_step(3, 4, got, pend, [], [first])
    x3, message = run_forward_step(4, 4, exchange(message), pend, [x2], [far, near])
    got = exchange(message)
    pend, (y2, y3), (first, d4, d5) = run_forward_rest(
        (2, 3), [x2, x3], pend, panels, inv_diag, ((5, 4), (4, 4), (5, 5))
    )
    x4, message = run_forward_step(5, 4, got, pend, [], [first])
    message = run_forward_last(exchange(message), [y0, y1, y2, y3], x4, d4, d5)
    y, message = run_backward_start(exchange(message, "leaf"), d5)
    s5, message = run_backward_next(exchange(message), y, d4, first)
    got = exchange(message)
    pend, (first, far, near) = run_backward_diag(y, s5, panels, inv_diag, ((4, 3), (4, 2), (3, 2)))
    s4, message = run_backward_step(3, got, pend, [], [first])
    s3, message = run_backward_step(2, exchange(message), pend, [s4], [far, near])
    got = exchange(message)
    pend, (first, far, near) = run_backward_rest((4, 3), [s4, s3], pend, panels, ((2, 1), (2, 0), (1, 0)))
    s2, message = run_backward_step(1, got, pend, [], [first])
    s1, message = run_backward_step(0, exchange(message), pend, [s2], [far, near])
    got = exchange(message)
    xs = [s1, s2, s3, s4, s5]
    rows, message = run_own_finish(place, got, xs, index)
    got = exchange(message)
    leaf_x = run_leaf_backward(live_rows, got, table, rank, leaf_y, leaf_inv, update_blocks)
    sep_solution = rows.reshape(V, LEVELS, 4, 1, 32)
    return leaf_x, sep_solution


def solution(mesh):
    in_specs = (
        P(ALL, None, None),
        P(ALL, None, None),
        P(ALL, None, None),
        P(ALL, None),
        P(ALL),
        P(None, None, None, "sep", None),
        P(None, None, "sep", None, "leaf"),
        P(None, None, "sep", None, "leaf"),
    )
    out_specs = (P(ALL, None, None), P(None, None, None, "sep", None))
    return jax.shard_map(per_device, mesh=mesh, in_specs=in_specs, out_specs=out_specs, check_vma=False)
```

```python
import functools

import jax
import jax.numpy as jnp
from jax import lax
from jax.experimental import pallas as pl
from jax.experimental.pallas import tpu as pltpu
from jax.sharding import PartitionSpec as P

F32 = jnp.float32
BF16 = jnp.bfloat16
V = 16
LEVELS = 6
ROWS = 128
COLS = 1024
UPD = 1024
CHUNKS = 2
ALL = ("leaf", "sep")
VMEM_LIMIT = 51 * 1024 * 1024
NT = (((1,), (1,)), ((), ()))
NN = (((1,), (0,)), ((), ()))


def pair_index(upper, lower):
    return lower * (LEVELS - 1) - lower * (lower - 1) // 2 + upper - lower - 1


def iota(shape, dim):
    return lax.broadcasted_iota(jnp.int32, shape, dim)


def dot(a, b, dims):
    return lax.dot_general(a, b, dims, preferred_element_type=F32)


def split(x):
    high = x.astype(BF16)
    return high, (x - high.astype(F32)).astype(BF16)


def product(x, w, dims):
    xh, xl = split(x)
    wh, wl = split(w)
    m = x.shape[0]
    both = dot(jnp.concatenate([xh, xl], 0), wh, dims)
    return both[:m] + both[m:] + dot(xh, wl, dims)


def exact_rows(x, onehot, dims):
    xh, xl = split(x)
    m = x.shape[0]
    both = dot(jnp.concatenate([xh, xl], 0), onehot, dims)
    return both[:m] + both[m:]


def block_swap(t):
    gap = (iota((16, 128), 1) // 32 - iota((16, 128), 0) // 4) & 3
    out = t
    for d in range(1, 4):
        moved = pltpu.roll(pltpu.roll(t, 32 * d, 1), 16 - 4 * d, 0)
        out = jnp.where(gap == d, moved, out)
    return out


def call(body, out_shape, in_specs, out_specs, scratch=(), flops=0, nbytes=0, limit=VMEM_LIMIT):
    return pl.pallas_call(
        body,
        out_shape=out_shape,
        in_specs=in_specs,
        out_specs=out_specs,
        scratch_shapes=scratch,
        compiler_params=pltpu.CompilerParams(vmem_limit_bytes=limit),
        cost_estimate=pl.CostEstimate(flops=flops, bytes_accessed=nbytes, transcendentals=0),
    )


def sds(shape, dtype=F32):
    return jax.ShapeDtypeStruct(shape, dtype)


VM = pl.BlockSpec(memory_space=pltpu.VMEM)
SMEM = pl.BlockSpec(memory_space=pltpu.SMEM)
ANY = pl.BlockSpec(memory_space=pl.ANY)
HBM = pl.BlockSpec(memory_space=pltpu.HBM)


def fetch(sources, buffer, sems):
    copies = [pltpu.make_async_copy(src, buffer.at[n], sems.at[n]) for n, src in enumerate(sources)]
    for one in copies:
        one.start()
    return copies


def leaf_forward(live_ref, rhs_hbm, map_hbm, inv_ref, upd_ref, y_ref, msg_ref, t_hbm, rank_hbm, t_ref, rank_ref, rhs_ref, map_ref, buffer, sems):
    step = UPD // CHUNKS
    small = [pltpu.make_async_copy(map_hbm, map_ref, sems.at[2 * CHUNKS]), pltpu.make_async_copy(rhs_hbm, rhs_ref, sems.at[2 * CHUNKS + 1])]
    for one in small:
        one.start()
    sources = []
    for n in range(CHUNKS):
        for ref in (inv_ref, upd_ref):
            sources.append(ref.at[0, pl.ds(step * n, step), :])
    copies = fetch(sources, buffer, sems)
    small[0].wait()
    rows = map_ref[...]
    owner = (rows >> 5) & 127
    hot = (iota((128, UPD), 0) == owner).astype(F32)
    ones = jnp.where((iota((128, 256), 0) < iota((128, 256), 1)), 1.0, 0.0).astype(BF16)
    carry = jnp.zeros((128, 128), F32)
    before = []
    for n in range(UPD // 128):
        counts = dot(hot[:, 128 * n : 128 * n + 128].astype(BF16), ones, NN)
        before.append(counts[:, :128] + carry)
        carry += counts[:, 128:]
    before = jnp.concatenate(before, 1)
    rank = jnp.sum(hot * before, axis=0, keepdims=True).astype(jnp.int32)
    rank_ref[...] = jnp.broadcast_to(rank, rank_ref.shape)
    for half in range(2):
        t_ref[pl.ds(128 * half, 128), :] = jnp.where((rank >> 3) == half, hot, 0.0).astype(BF16)
    tables = [
        pltpu.make_async_copy(t_ref, t_hbm, sems.at[2 * CHUNKS + 2]),
        pltpu.make_async_copy(rank_ref, rank_hbm, sems.at[2 * CHUNKS + 3]),
    ]
    for one in tables:
        one.start()
    live = iota((1, UPD), 1) < live_ref[0]
    local = (rows >> 12) * 32 + (rows & 31) + 1
    places = jnp.where((iota((128, UPD), 0) == rank) & live, local.astype(F32), 0.0)
    msg_ref[pl.ds(2, 128, 4), :] = dot(hot.astype(BF16), places.astype(BF16), NT)
    msg_ref[pl.ds(3, 128, 4), :] = jnp.zeros((128, 128), F32)
    acc = jnp.zeros((V, UPD), F32)
    small[1].wait()
    for n in range(CHUNKS):
        copies[2 * n].wait()
        y_part = product(rhs_ref[0], buffer[2 * n], NT)
        y_ref[:, step * n : step * n + step] = y_part
        copies[2 * n + 1].wait()
        acc += product(y_part, buffer[2 * n + 1], NN)
    group = iota((128, UPD), 0) >> 4
    spread = jnp.where((group == (rank & 7)) & live, jnp.concatenate([acc] * 8, 0), 0.0)
    parts = jnp.concatenate(split(spread), 0)
    for half in range(2):
        got = dot(t_ref[pl.ds(128 * half, 128), :], parts, NT)
        msg_ref[pl.ds(half, 128, 4), :] = got[:, :128] + got[:, 128:]
    for one in tables:
        one.wait()


def run_leaf_forward(live, rhs, rows, inv, upd):
    return call(
        leaf_forward,
        (sds((V, UPD)), sds((512, 128)), sds((256, UPD), BF16), sds((8, UPD), jnp.int32)),
        [SMEM, HBM, HBM, HBM, HBM],
        (VM, VM, HBM, HBM),
        scratch=[
            pltpu.VMEM((256, UPD), BF16),
            pltpu.VMEM((8, UPD), jnp.int32),
            pltpu.VMEM((1, V, 1024), F32),
            pltpu.VMEM((1, UPD), jnp.int32),
            pltpu.VMEM((2 * CHUNKS, UPD // CHUNKS, 1024), F32),
            pltpu.SemaphoreType.DMA((2 * CHUNKS + 4,)),
        ],
        flops=2 * 16 * 3 * (2 << 20),
        nbytes=8 << 20,
        limit=60 * 1024 * 1024,
    )(live, rhs, rows, inv, upd)


def leaf_backward(live_ref, got_ref, t_ref, rank_ref, y_ref, inv_ref, upd_ref, out_ref, buffer, sems):
    step = UPD // CHUNKS
    sources = []
    for n in range(CHUNKS):
        for ref in (upd_ref, inv_ref):
            sources.append(ref.at[0, pl.ds(step * n, step), :])
    copies = fetch(sources, buffer, sems)
    live = iota((1, UPD), 1) < live_ref[0]
    group = iota((128, UPD), 0) >> 4
    total = jnp.zeros((128, UPD), F32)
    for half in range(2):
        values = got_ref[pl.ds(half, 128, 2), :].T
        total += exact_rows(values, t_ref[pl.ds(128 * half, 128), :], NN)
    total = jnp.where((group == (rank_ref[0:1, :] & 7)) & live, total, 0.0)
    mapped = total[0:16]
    for g in range(1, 8):
        mapped += total[16 * g : 16 * g + 16]
    out = jnp.zeros((V, 1024), F32)
    for n in range(CHUNKS):
        copies[2 * n].wait()
        z = y_ref[:, step * n : step * n + step] - product(mapped, buffer[2 * n], NT)
        copies[2 * n + 1].wait()
        out += product(z, buffer[2 * n + 1], NN)
    out_ref[0] = out


def run_leaf_backward(live, got, t, rank, y, inv, upd):
    return call(
        leaf_backward,
        sds((1, V, 1024)),
        [SMEM, VM, VM, VM, VM, HBM, HBM],
        VM,
        scratch=[pltpu.VMEM((2 * CHUNKS, UPD // CHUNKS, 1024), F32), pltpu.SemaphoreType.DMA((2 * CHUNKS,))],
        flops=2 * 16 * 3 * (2 << 20),
        nbytes=8 << 20,
    )(live, got, t, rank, y, inv, upd)


def own_start(place_ref, got_ref, rhs_ref, after_ref, pend_ref, msg_ref, index_ref):
    values = [got_ref[pl.ds(half, 128, 4), :].T for half in range(2)]
    index = got_ref[pl.ds(2, 128, 4), :]
    index_ref[...] = index
    column = (iota((128, 256), 1) + 1).astype(F32)
    hot, rows = [], []
    for half in range(2):
        for g in range(8):
            j = 8 * half + g
            hot.append(jnp.where(index[:, j : j + 1] == column, 1.0, 0.0).astype(BF16))
            rows.append(values[half][16 * g : 16 * g + 16])
    total = exact_rows(jnp.concatenate(rows, 1), jnp.concatenate(hot, 0), NN)
    mine = iota((V, 128), 1) // 32 == place_ref[0]
    first = None
    for k in range(LEVELS):
        one = total[:, 32 * k : 32 * k + 32]
        row = jnp.where(mine, rhs_ref[:, 128 * k : 128 * k + 128] - jnp.concatenate([one] * 4, 1), 0.0)
        pend_ref[k] = row
        if k == 0:
            first = row
    turned = block_swap(first)
    chunk = turned[0:4] + turned[4:8] + turned[8:12] + turned[12:16]
    msg_ref[...] = jnp.concatenate([chunk] * 32, 0)


def run_own_start(place, got, rhs, after):
    return call(
        own_start,
        (sds((LEVELS, V, 128)), sds((128, 128)), sds((128, 128))),
        [SMEM, VM, VM, ANY],
        (VM, VM, VM),
        flops=1 << 27,
        nbytes=1 << 19,
    )(place, got, rhs, after)


def columns_of(got_ref, parts):
    total = got_ref[pl.ds(0, 128), :]
    for p in range(1, parts):
        total += got_ref[pl.ds(128 * p, 128), :]
    return jnp.concatenate([block_swap(total[16 * t : 16 * t + 16]) for t in range(8)], 1)


def row_message(msg_ref, rows):
    turned = block_swap(rows)
    for q in range(4):
        msg_ref[pl.ds(128 * q, 128), :] = jnp.concatenate([turned[4 * q : 4 * q + 4]] * 32, 0)


def block_parts(block):
    return jnp.concatenate(split(block.reshape(ROWS, COLS)), 0)


def times_columns(x, w):
    out = dot(jnp.concatenate(split(x), 0), w, NT)
    return (out[:V, :ROWS] + out[V:, :ROWS]) + (out[:V, ROWS:] + out[V:, ROWS:])


def times_rows(x, w):
    half = jnp.concatenate(split(x), 0)
    out = dot(jnp.concatenate([half, half], 1), w, NN)
    return out[:V] + out[V:]


PARTS = (2 * ROWS, COLS)


def buffers(count):
    return [pltpu.VMEM((count, 4, 32, COLS), F32), pltpu.SemaphoreType.DMA((count,))]


def block_of(panels_ref, diag_ref, upper, lower):
    return diag_ref.at[lower, :, 0] if upper == lower else panels_ref.at[pair_index(upper, lower), :, 0]


FIRST = ((1, 0), (2, 0), (2, 1))


def first_blocks(after_ref, panels_ref, *refs):
    w_refs, (buffer, sems) = refs[:-2], refs[-2:]
    copies = fetch([block_of(panels_ref, None, *pair) for pair in FIRST], buffer, sems)
    for n, w_ref in enumerate(w_refs):
        copies[n].wait()
        w_ref[...] = block_parts(buffer[n])


def run_first_blocks(after, panels):
    n = len(FIRST)
    return call(
        first_blocks,
        [sds(PARTS, BF16)] * n,
        [ANY, HBM],
        [VM] * n,
        scratch=buffers(n),
        flops=n << 20,
        nbytes=n << 20,
    )(after, panels)


def forward_step(level, parts, count, *refs):
    got_ref, pend_ref = refs[:2]
    earlier, blocks, (x_ref, msg_ref) = refs[2 : 1 + count], refs[1 + count : 1 + 2 * count], refs[-2:]
    x = columns_of(got_ref, parts)
    x_ref[...] = x
    rows = pend_ref[level]
    for one, w_ref in zip([r[...] for r in earlier] + [x], blocks):
        rows -= times_columns(one, w_ref[...])
    row_message(msg_ref, rows)


def run_forward_step(level, parts, got, pend, earlier, blocks):
    return call(
        functools.partial(forward_step, level, parts, len(blocks)),
        (sds((V, COLS)), sds((512, 128))),
        [VM] * (2 + len(earlier) + len(blocks)),
        (VM, VM),
        flops=len(blocks) << 24,
        nbytes=len(blocks) << 20,
    )(got, pend, *earlier, *blocks)


def forward_rest(levels, wanted, *refs):
    n = len(levels)
    x_refs, (pend_ref, panels_ref, diag_ref), refs = refs[:n], refs[n : n + 3], refs[n + 3 :]
    out_ref, y_refs, w_refs, (buffer, sems) = refs[0], refs[1 : 1 + n], refs[1 + n : -2], refs[-2:]
    later = range(levels[-1] + 2, LEVELS)
    pairs = [(j, k) for j in later for k in levels] + [(k, k) for k in levels] + list(wanted)
    copies = fetch([block_of(panels_ref, diag_ref, *pair) for pair in pairs], buffer, sems)
    out_ref[...] = pend_ref[...]
    slot = 0
    for j in later:
        rows = pend_ref[j]
        for x_ref in x_refs:
            copies[slot].wait()
            rows -= times_columns(x_ref[...], block_parts(buffer[slot]))
            slot += 1
        out_ref[j] = rows
    for x_ref, y_ref in zip(x_refs, y_refs):
        copies[slot].wait()
        y_ref[...] = times_columns(x_ref[...], block_parts(buffer[slot]))
        slot += 1
    for w_ref in w_refs:
        copies[slot].wait()
        w_ref[...] = block_parts(buffer[slot])
        slot += 1


def run_forward_rest(levels, xs, pend, panels, diag, wanted):
    n = len(levels)
    count = n * (LEVELS - 1 - levels[-1]) + len(wanted)
    out = call(
        functools.partial(forward_rest, levels, wanted),
        (sds((LEVELS, V, 128)), *[sds((V, 128))] * n, *[sds(PARTS, BF16)] * len(wanted)),
        [VM] * n + [VM, HBM, HBM],
        (VM,) * (1 + n + len(wanted)),
        scratch=buffers(count),
        flops=count << 24,
        nbytes=count << 19,
    )(*xs, pend, panels, diag)
    return out[0], out[1 : 1 + n], out[1 + n :]


def forward_last(got_ref, y0, y1, y2, y3, x4_ref, w4_ref, w5_ref, msg_ref):
    y4 = times_columns(x4_ref[...], w4_ref[...])
    y5 = times_columns(columns_of(got_ref, 4), w5_ref[...])
    for l in range(4):
        for k, one in enumerate((y0, y1, y2, y3)):
            msg_ref[pl.ds(96 * l + 16 * k, 16), :] = one[...]
        msg_ref[pl.ds(96 * l + 64, 16), :] = y4
        msg_ref[pl.ds(96 * l + 80, 16), :] = y5


def run_forward_last(got, ys, x4, w4, w5):
    return call(
        forward_last,
        sds((4 * 96, 128)),
        [VM] * 8,
        VM,
        flops=2 << 24,
        nbytes=1 << 20,
    )(got, *ys, x4, w4, w5)


def column_message(msg_ref, columns, copies=4):
    for t in range(8):
        turned = block_swap(columns[:, 128 * t : 128 * t + 128])
        for l in range(copies):
            msg_ref[pl.ds(128 * l + 16 * t, 16), :] = turned


def backward_start(got_ref, w_ref, y_ref, msg_ref):
    y = got_ref[pl.ds(0, 96), :]
    for l in range(1, 4):
        y += got_ref[pl.ds(96 * l, 96), :]
    y_ref[...] = y
    column_message(msg_ref, times_rows(y[80:96], w_ref[...]))


def run_backward_start(got, w):
    return call(
        backward_start,
        (sds((96, 128)), sds((512, 128))),
        [VM, VM],
        (VM, VM),
        flops=1 << 24,
        nbytes=1 << 20,
    )(got, w)


def rows_of(got_ref):
    parts = []
    for q in range(4):
        total = got_ref[pl.ds(128 * q, 8), :]
        for t in range(1, 16):
            total += got_ref[pl.ds(128 * q + 8 * t, 8), :]
        parts.append(total[0:4] + total[4:8])
    return block_swap(jnp.concatenate(parts, 0))


def backward_step(level, count, *refs):
    got_ref, pend_ref = refs[:2]
    earlier, blocks, (x_ref, msg_ref) = refs[2 : 1 + count], refs[1 + count : 1 + 2 * count], refs[-2:]
    x = rows_of(got_ref)
    x_ref[...] = x
    columns = pend_ref[level]
    for one, w_ref in zip([r[...] for r in earlier] + [x], blocks):
        columns -= times_rows(one, w_ref[...])
    column_message(msg_ref, columns, 4 if level else 1)


def run_backward_step(level, got, pend, earlier, blocks):
    return call(
        functools.partial(backward_step, level, len(blocks)),
        (sds((V, 128)), sds((512 if level else 128, 128))),
        [VM] * (2 + len(earlier) + len(blocks)),
        (VM, VM),
        flops=len(blocks) << 24,
        nbytes=len(blocks) << 20,
    )(got, pend, *earlier, *blocks)


def backward_next(got_ref, y_ref, diag_ref, w_ref, x_ref, msg_ref):
    x = rows_of(got_ref)
    x_ref[...] = x
    column_message(msg_ref, times_rows(y_ref[64:80, :], diag_ref[...]) - times_rows(x, w_ref[...]))


def run_backward_next(got, y, diag, w):
    return call(
        backward_next,
        (sds((V, 128)), sds((512, 128))),
        [VM] * 4,
        (VM, VM),
        flops=2 << 24,
        nbytes=1 << 20,
    )(got, y, diag, w)


def backward_diag(wanted, y_ref, x_ref, panels_ref, diag_ref, out_ref, *refs):
    w_refs, (buffer, sems) = refs[:-2], refs[-2:]
    pairs = [(up, k) for k in range(LEVELS - 2) for up in (k, LEVELS - 1)] + list(wanted)
    copies = fetch([block_of(panels_ref, diag_ref, *pair) for pair in pairs], buffer, sems)
    for k in range(LEVELS - 2):
        copies[2 * k].wait()
        columns = times_rows(y_ref[pl.ds(16 * k, 16), :], block_parts(buffer[2 * k]))
        copies[2 * k + 1].wait()
        out_ref[k] = columns - times_rows(x_ref[...], block_parts(buffer[2 * k + 1]))
    for n, w_ref in enumerate(w_refs):
        slot = 2 * (LEVELS - 2) + n
        copies[slot].wait()
        w_ref[...] = block_parts(buffer[slot])


def run_backward_diag(y, x, panels, diag, wanted):
    out = call(
        functools.partial(backward_diag, wanted),
        (sds((LEVELS - 2, V, COLS)), *[sds(PARTS, BF16)] * len(wanted)),
        [VM, VM, HBM, HBM],
        (VM,) * (1 + len(wanted)),
        scratch=buffers(2 * (LEVELS - 2) + len(wanted)),
        flops=11 << 24,
        nbytes=6 << 20,
    )(y, x, panels, diag)
    return out[0], out[1:]


def backward_rest(levels, wanted, *refs):
    n = len(levels)
    x_refs, (pend_ref, panels_ref), refs = refs[:n], refs[n : n + 2], refs[n + 2 :]
    out_ref, w_refs, (buffer, sems) = refs[0], refs[1:-2], refs[-2:]
    lower = range(levels[-1] - 2, -1, -1)
    pairs = [(k, j) for j in lower for k in levels] + list(wanted)
    copies = fetch([block_of(panels_ref, None, *pair) for pair in pairs], buffer, sems)
    slot = 0
    for j in lower:
        columns = pend_ref[j]
        for x_ref in x_refs:
            copies[slot].wait()
            columns -= times_rows(x_ref[...], block_parts(buffer[slot]))
            slot += 1
        out_ref[j] = columns
    for w_ref in w_refs:
        copies[slot].wait()
        w_ref[...] = block_parts(buffer[slot])
        slot += 1


def run_backward_rest(levels, xs, pend, panels, wanted):
    n, lower = len(levels), levels[-1] - 1
    count = n * lower + len(wanted)
    out = call(
        functools.partial(backward_rest, levels, wanted),
        (sds((lower, V, COLS)), *[sds(PARTS, BF16)] * len(wanted)),
        [VM] * n + [VM, HBM],
        (VM,) * (1 + len(wanted)),
        scratch=buffers(count),
        flops=count << 24,
        nbytes=count << 19,
    )(*xs, pend, panels)
    return out[0], out[1:]


def own_finish(place_ref, got_ref, x1, x2, x3, x4, x5, index_ref, chunk_ref, msg_ref):
    total = got_ref[pl.ds(0, 8), :]
    for t in range(1, 16):
        total += got_ref[pl.ds(8 * t, 8), :]
    chunk = total[0:4] + total[4:8]
    chunk_ref[...] = jnp.concatenate([chunk] * 2, 0)
    mine = [block_swap(jnp.concatenate([chunk] * 4, 0))[:, :32]]
    for x in [r[...] for r in (x1, x2, x3, x4, x5)]:
        one = jnp.zeros((V, 32), F32)
        for q in range(4):
            one = jnp.where(place_ref[0] == q, x[:, 32 * q : 32 * q + 32], one)
        mine.append(one)
    rows = jnp.concatenate(mine + [jnp.zeros((V, 64), F32)], 1)
    high, low = split(jnp.concatenate([rows] * 8, 0))
    table = jnp.concatenate([high, low], 0).astype(F32)
    index = index_ref[...]
    column = (iota((128, 256), 1) + 1).astype(F32)
    group = (iota((256, 256), 0) >> 4) & 7
    hot, tables = [], []
    for g in range(8):
        pair = [jnp.where(index[:, j : j + 1] == column, 1.0, 0.0) for j in (g, 8 + g)]
        hot.append(jnp.concatenate(pair, 0).astype(BF16))
        tables.append(jnp.where(group == g, table, 0.0).astype(BF16))
    got = dot(jnp.concatenate(hot, 1), jnp.concatenate(tables, 1), NT)
    for half in range(2):
        part = got[128 * half : 128 * half + 128]
        msg_ref[pl.ds(half, 128, 2), :] = part[:, :128] + part[:, 128:]


def run_own_finish(place, got, xs, index):
    return call(
        own_finish,
        (sds((8, 128)), sds((256, 128))),
        [SMEM, VM] + [VM] * 5 + [VM],
        (VM, VM),
        flops=1 << 27,
        nbytes=1 << 20,
    )(place, got, *xs, index)


def write_rows(place_ref, c0, c1, c2, c3, x1, x2, x3, x4, x5, out_ref):
    chunks = [r[0:4, :] for r in (c0, c1, c2, c3)]
    parts = []
    for q in range(4):
        one = jnp.zeros((4, 128), F32)
        for d in range(4):
            one = jnp.where(((place_ref[0] + d) & 3) == q, chunks[d], one)
        parts.append(one)
    for k, x in enumerate([block_swap(jnp.concatenate(parts, 0))] + [r[...] for r in (x1, x2, x3, x4, x5)]):
        for q in range(4):
            out_ref[pl.ds(4 * k + q, V, 4 * LEVELS), :] = x[:, 32 * q : 32 * q + 32]


def run_write_rows(place, chunks, xs):
    return call(
        write_rows,
        sds((V * LEVELS * 4, 32)),
        [SMEM] + [VM] * 9,
        VM,
        flops=1 << 20,
        nbytes=1 << 18,
    )(place, *chunks, *xs)


def exchange(message, axis=ALL):
    return lax.all_to_all(message, axis, 0, 0, tiled=True)


def per_device(leaf_rhs, leaf_inv, update_blocks, row_map, live_rows, sep_rhs, inv_diag, panels):
    place = lax.axis_index("leaf").astype(jnp.int32).reshape(1)
    rhs = sep_rhs.reshape(V, LEVELS * 128)
    leaf_y, message, table, rank = run_leaf_forward(live_rows, leaf_rhs, row_map, leaf_inv, update_blocks)
    got = exchange(message)
    first, far, near = run_first_blocks(leaf_y, panels)
    pend, message, index = run_own_start(place, got, rhs, near)
    got = exchange(message, "sep")
    x0, message = run_forward_step(1, 1, got, pend, [], [first])
    x1, message = run_forward_step(2, 4, exchange(message), pend, [x0], [far, near])
    got = exchange(message)
    pend, (y0, y1), (first, far, near) = run_forward_rest(
        (0, 1), [x0, x1], pend, panels, inv_diag, ((3, 2), (4, 2), (4, 3))
    )
    x2, message = run_forward_step(3, 4, got, pend, [], [first])
    x3, message = run_forward_step(4, 4, exchange(message), pend, [x2], [far, near])
    got = exchange(message)
    pend, (y2, y3), (first, d4, d5) = run_forward_rest(
        (2, 3), [x2, x3], pend, panels, inv_diag, ((5, 4), (4, 4), (5, 5))
    )
    x4, message = run_forward_step(5, 4, got, pend, [], [first])
    message = run_forward_last(exchange(message), [y0, y1, y2, y3], x4, d4, d5)
    y, message = run_backward_start(exchange(message, "leaf"), d5)
    s5, message = run_backward_next(exchange(message), y, d4, first)
    got = exchange(message)
    pend, (first, far, near) = run_backward_diag(y, s5, panels, inv_diag, ((4, 3), (4, 2), (3, 2)))
    s4, message = run_backward_step(3, got, pend, [], [first])
    s3, message = run_backward_step(2, exchange(message), pend, [s4], [far, near])
    got = exchange(message)
    pend, (first, far, near) = run_backward_rest((4, 3), [s4, s3], pend, panels, ((2, 1), (2, 0), (1, 0)))
    s2, message = run_backward_step(1, got, pend, [], [first])
    s1, message = run_backward_step(0, exchange(message), pend, [s2], [far, near])
    xs = [s1, s2, s3, s4, s5]
    chunk, message = run_own_finish(place, exchange(message, "sep"), xs, index)
    got = exchange(message)
    chunks = [chunk]
    for d in range(1, 4):
        chunks.append(lax.ppermute(chunk, "leaf", [((l + d) % 4, l) for l in range(4)]))
    rows = run_write_rows(place, chunks, xs)
    leaf_x = run_leaf_backward(live_rows, got, table, rank, leaf_y, leaf_inv, update_blocks)
    sep_solution = rows.reshape(V, LEVELS, 4, 1, 32)
    return leaf_x, sep_solution


def solution(mesh):
    in_specs = (
        P(ALL, None, None),
        P(ALL, None, None),
        P(ALL, None, None),
        P(ALL, None),
        P(ALL),
        P(None, None, None, "sep", None),
        P(None, None, "sep", None, "leaf"),
        P(None, None, "sep", None, "leaf"),
    )
    out_specs = (P(ALL, None, None), P(None, None, None, "sep", None))
    return jax.shard_map(per_device, mesh=mesh, in_specs=in_specs, out_specs=out_specs, check_vma=False)
```

```python
import functools

import jax
import jax.numpy as jnp
from jax import lax
from jax.experimental import pallas as pl
from jax.experimental.pallas import tpu as pltpu
from jax.sharding import PartitionSpec as P

F32 = jnp.float32
BF16 = jnp.bfloat16
V = 16
LEVELS = 6
ROWS = 128
COLS = 1024
UPD = 1024
CHUNKS = 2
ALL = ("leaf", "sep")
VMEM_LIMIT = 51 * 1024 * 1024
NT = (((1,), (1,)), ((), ()))
NN = (((1,), (0,)), ((), ()))


def pair_index(upper, lower):
    return lower * (LEVELS - 1) - lower * (lower - 1) // 2 + upper - lower - 1


def iota(shape, dim):
    return lax.broadcasted_iota(jnp.int32, shape, dim)


def dot(a, b, dims):
    return lax.dot_general(a, b, dims, preferred_element_type=F32)


def split(x):
    high = x.astype(BF16)
    return high, (x - high.astype(F32)).astype(BF16)


def product(x, w, dims):
    xh, xl = split(x)
    wh, wl = split(w)
    m = x.shape[0]
    both = dot(jnp.concatenate([xh, xl], 0), wh, dims)
    return both[:m] + both[m:] + dot(xh, wl, dims)


def exact_rows(x, onehot, dims):
    xh, xl = split(x)
    m = x.shape[0]
    both = dot(jnp.concatenate([xh, xl], 0), onehot, dims)
    return both[:m] + both[m:]


def block_swap(t):
    gap = (iota((16, 128), 1) // 32 - iota((16, 128), 0) // 4) & 3
    out = t
    for d in range(1, 4):
        moved = pltpu.roll(pltpu.roll(t, 32 * d, 1), 16 - 4 * d, 0)
        out = jnp.where(gap == d, moved, out)
    return out


def call(body, out_shape, in_specs, out_specs, scratch=(), flops=0, nbytes=0, limit=VMEM_LIMIT):
    return pl.pallas_call(
        body,
        out_shape=out_shape,
        in_specs=in_specs,
        out_specs=out_specs,
        scratch_shapes=scratch,
        compiler_params=pltpu.CompilerParams(vmem_limit_bytes=limit),
        cost_estimate=pl.CostEstimate(flops=flops, bytes_accessed=nbytes, transcendentals=0),
    )


def sds(shape, dtype=F32):
    return jax.ShapeDtypeStruct(shape, dtype)


VM = pl.BlockSpec(memory_space=pltpu.VMEM)
SMEM = pl.BlockSpec(memory_space=pltpu.SMEM)
ANY = pl.BlockSpec(memory_space=pl.ANY)
HBM = pl.BlockSpec(memory_space=pltpu.HBM)


def fetch(sources, buffer, sems):
    copies = [pltpu.make_async_copy(src, buffer.at[n], sems.at[n]) for n, src in enumerate(sources)]
    for one in copies:
        one.start()
    return copies


def leaf_forward(live_ref, rhs_hbm, map_hbm, inv_ref, upd_ref, y_ref, msg_ref, t_hbm, rank_hbm, t_ref, rank_ref, rhs_ref, map_ref, buffer, sems):
    step = UPD // CHUNKS
    small = [pltpu.make_async_copy(map_hbm, map_ref, sems.at[2 * CHUNKS]), pltpu.make_async_copy(rhs_hbm, rhs_ref, sems.at[2 * CHUNKS + 1])]
    for one in small:
        one.start()
    sources = []
    for n in range(CHUNKS):
        for ref in (inv_ref, upd_ref):
            sources.append(ref.at[0, pl.ds(step * n, step), :])
    copies = fetch(sources, buffer, sems)
    small[0].wait()
    rows = map_ref[...]
    owner = (rows >> 5) & 127
    hot = (iota((128, UPD), 0) == owner).astype(F32)
    ones = jnp.where((iota((128, 256), 0) < iota((128, 256), 1)), 1.0, 0.0).astype(BF16)
    carry = jnp.zeros((128, 128), F32)
    before = []
    for n in range(UPD // 128):
        counts = dot(hot[:, 128 * n : 128 * n + 128].astype(BF16), ones, NN)
        before.append(counts[:, :128] + carry)
        carry += counts[:, 128:]
    before = jnp.concatenate(before, 1)
    rank = jnp.sum(hot * before, axis=0, keepdims=True).astype(jnp.int32)
    rank_ref[...] = jnp.broadcast_to(rank, rank_ref.shape)
    for half in range(2):
        t_ref[pl.ds(128 * half, 128), :] = jnp.where((rank >> 3) == half, hot, 0.0).astype(BF16)
    tables = [
        pltpu.make_async_copy(t_ref, t_hbm, sems.at[2 * CHUNKS + 2]),
        pltpu.make_async_copy(rank_ref, rank_hbm, sems.at[2 * CHUNKS + 3]),
    ]
    for one in tables:
        one.start()
    live = iota((1, UPD), 1) < live_ref[0]
    local = (rows >> 12) * 32 + (rows & 31) + 1
    places = jnp.where((iota((128, UPD), 0) == rank) & live, local.astype(F32), 0.0)
    msg_ref[pl.ds(2, 128, 4), :] = dot(hot.astype(BF16), places.astype(BF16), NT)
    msg_ref[pl.ds(3, 128, 4), :] = jnp.zeros((128, 128), F32)
    acc = jnp.zeros((V, UPD), F32)
    small[1].wait()
    for n in range(CHUNKS):
        copies[2 * n].wait()
        y_part = product(rhs_ref[0], buffer[2 * n], NT)
        y_ref[:, step * n : step * n + step] = y_part
        copies[2 * n + 1].wait()
        acc += product(y_part, buffer[2 * n + 1], NN)
    group = iota((128, UPD), 0) >> 4
    spread = jnp.where((group == (rank & 7)) & live, jnp.concatenate([acc] * 8, 0), 0.0)
    parts = jnp.concatenate(split(spread), 0)
    for half in range(2):
        got = dot(t_ref[pl.ds(128 * half, 128), :], parts, NT)
        msg_ref[pl.ds(half, 128, 4), :] = got[:, :128] + got[:, 128:]
    for one in tables:
        one.wait()


def run_leaf_forward(live, rhs, rows, inv, upd):
    return call(
        leaf_forward,
        (sds((V, UPD)), sds((512, 128)), sds((256, UPD), BF16), sds((8, UPD), jnp.int32)),
        [SMEM, HBM, HBM, HBM, HBM],
        (VM, VM, HBM, HBM),
        scratch=[
            pltpu.VMEM((256, UPD), BF16),
            pltpu.VMEM((8, UPD), jnp.int32),
            pltpu.VMEM((1, V, 1024), F32),
            pltpu.VMEM((1, UPD), jnp.int32),
            pltpu.VMEM((2 * CHUNKS, UPD // CHUNKS, 1024), F32),
            pltpu.SemaphoreType.DMA((2 * CHUNKS + 4,)),
        ],
        flops=2 * 16 * 3 * (2 << 20),
        nbytes=8 << 20,
        limit=60 * 1024 * 1024,
    )(live, rhs, rows, inv, upd)


def leaf_backward(live_ref, got_ref, t_ref, rank_ref, y_ref, inv_ref, upd_ref, out_ref, buffer, sems):
    step = UPD // CHUNKS
    sources = []
    for n in range(CHUNKS):
        for ref in (upd_ref, inv_ref):
            sources.append(ref.at[0, pl.ds(step * n, step), :])
    copies = fetch(sources, buffer, sems)
    live = iota((1, UPD), 1) < live_ref[0]
    group = iota((128, UPD), 0) >> 4
    total = jnp.zeros((128, UPD), F32)
    for half in range(2):
        values = got_ref[pl.ds(half, 128, 2), :].T
        total += exact_rows(values, t_ref[pl.ds(128 * half, 128), :], NN)
    total = jnp.where((group == (rank_ref[0:1, :] & 7)) & live, total, 0.0)
    mapped = total[0:16]
    for g in range(1, 8):
        mapped += total[16 * g : 16 * g + 16]
    out = jnp.zeros((V, 1024), F32)
    for n in range(CHUNKS):
        copies[2 * n].wait()
        z = y_ref[:, step * n : step * n + step] - product(mapped, buffer[2 * n], NT)
        copies[2 * n + 1].wait()
        out += product(z, buffer[2 * n + 1], NN)
    out_ref[0] = out


def run_leaf_backward(live, got, t, rank, y, inv, upd):
    return call(
        leaf_backward,
        sds((1, V, 1024)),
        [SMEM, VM, VM, VM, VM, HBM, HBM],
        VM,
        scratch=[pltpu.VMEM((2 * CHUNKS, UPD // CHUNKS, 1024), F32), pltpu.SemaphoreType.DMA((2 * CHUNKS,))],
        flops=2 * 16 * 3 * (2 << 20),
        nbytes=8 << 20,
    )(live, got, t, rank, y, inv, upd)


def own_start(place_ref, got_ref, rhs_ref, after_ref, pend_ref, msg_ref, index_ref):
    values = [got_ref[pl.ds(half, 128, 4), :].T for half in range(2)]
    index = got_ref[pl.ds(2, 128, 4), :]
    index_ref[...] = index
    column = (iota((128, 256), 1) + 1).astype(F32)
    hot, rows = [], []
    for half in range(2):
        for g in range(8):
            j = 8 * half + g
            hot.append(jnp.where(index[:, j : j + 1] == column, 1.0, 0.0).astype(BF16))
            rows.append(values[half][16 * g : 16 * g + 16])
    total = exact_rows(jnp.concatenate(rows, 1), jnp.concatenate(hot, 0), NN)
    mine = iota((V, 128), 1) // 32 == place_ref[0]
    first = None
    for k in range(LEVELS):
        one = total[:, 32 * k : 32 * k + 32]
        row = jnp.where(mine, rhs_ref[:, 128 * k : 128 * k + 128] - jnp.concatenate([one] * 4, 1), 0.0)
        pend_ref[k] = row
        if k == 0:
            first = row
    turned = block_swap(first)
    chunk = turned[0:4] + turned[4:8] + turned[8:12] + turned[12:16]
    msg_ref[...] = jnp.concatenate([chunk] * 32, 0)


def run_own_start(place, got, rhs, after):
    return call(
        own_start,
        (sds((LEVELS, V, 128)), sds((128, 128)), sds((128, 128))),
        [SMEM, VM, VM, ANY],
        (VM, VM, VM),
        flops=1 << 27,
        nbytes=1 << 19,
    )(place, got, rhs, after)


def columns_of(got_ref, parts):
    total = got_ref[pl.ds(0, 128), :]
    for p in range(1, parts):
        total += got_ref[pl.ds(128 * p, 128), :]
    return jnp.concatenate([block_swap(total[16 * t : 16 * t + 16]) for t in range(8)], 1)


def row_message(msg_ref, rows):
    turned = block_swap(rows)
    for q in range(4):
        msg_ref[pl.ds(128 * q, 128), :] = jnp.concatenate([turned[4 * q : 4 * q + 4]] * 32, 0)


def block_parts(block):
    return jnp.concatenate(split(block.reshape(ROWS, COLS)), 0)


def times_columns(x, w):
    out = dot(jnp.concatenate(split(x), 0), w, NT)
    return (out[:V, :ROWS] + out[V:, :ROWS]) + (out[:V, ROWS:] + out[V:, ROWS:])


def times_rows(x, w):
    half = jnp.concatenate(split(x), 0)
    out = dot(jnp.concatenate([half, half], 1), w, NN)
    return out[:V] + out[V:]


PARTS = (2 * ROWS, COLS)


def buffers(count):
    return [pltpu.VMEM((count, 4, 32, COLS), F32), pltpu.SemaphoreType.DMA((count,))]


def block_of(panels_ref, diag_ref, upper, lower):
    return diag_ref.at[lower, :, 0] if upper == lower else panels_ref.at[pair_index(upper, lower), :, 0]


FIRST = ((1, 0), (2, 0), (2, 1))


def first_blocks(after_ref, panels_ref, *refs):
    w_refs, (buffer, sems) = refs[:-2], refs[-2:]
    copies = fetch([block_of(panels_ref, None, *pair) for pair in FIRST], buffer, sems)
    for n, w_ref in enumerate(w_refs):
        copies[n].wait()
        w_ref[...] = block_parts(buffer[n])


def run_first_blocks(after, panels):
    n = len(FIRST)
    return call(
        first_blocks,
        [sds(PARTS, BF16)] * n,
        [ANY, HBM],
        [VM] * n,
        scratch=buffers(n),
        flops=n << 20,
        nbytes=n << 20,
    )(after, panels)


def forward_step(level, parts, count, *refs):
    got_ref, pend_ref = refs[:2]
    earlier, blocks, (x_ref, msg_ref) = refs[2 : 1 + count], refs[1 + count : 1 + 2 * count], refs[-2:]
    x = columns_of(got_ref, parts)
    x_ref[...] = x
    rows = pend_ref[level]
    for one, w_ref in zip([r[...] for r in earlier] + [x], blocks):
        rows -= times_columns(one, w_ref[...])
    row_message(msg_ref, rows)


def run_forward_step(level, parts, got, pend, earlier, blocks):
    return call(
        functools.partial(forward_step, level, parts, len(blocks)),
        (sds((V, COLS)), sds((512, 128))),
        [VM] * (2 + len(earlier) + len(blocks)),
        (VM, VM),
        flops=len(blocks) << 24,
        nbytes=len(blocks) << 20,
    )(got, pend, *earlier, *blocks)


def forward_rest(levels, wanted, *refs):
    n = len(levels)
    x_refs, (pend_ref, panels_ref, diag_ref), refs = refs[:n], refs[n : n + 3], refs[n + 3 :]
    out_ref, y_refs, w_refs, (buffer, sems) = refs[0], refs[1 : 1 + n], refs[1 + n : -2], refs[-2:]
    later = range(levels[-1] + 2, LEVELS)
    pairs = [(j, k) for j in later for k in levels] + [(k, k) for k in levels] + list(wanted)
    copies = fetch([block_of(panels_ref, diag_ref, *pair) for pair in pairs], buffer, sems)
    out_ref[...] = pend_ref[...]
    slot = 0
    for j in later:
        rows = pend_ref[j]
        for x_ref in x_refs:
            copies[slot].wait()
            rows -= times_columns(x_ref[...], block_parts(buffer[slot]))
            slot += 1
        out_ref[j] = rows
    for x_ref, y_ref in zip(x_refs, y_refs):
        copies[slot].wait()
        y_ref[...] = times_columns(x_ref[...], block_parts(buffer[slot]))
        slot += 1
    for w_ref in w_refs:
        copies[slot].wait()
        w_ref[...] = block_parts(buffer[slot])
        slot += 1


def run_forward_rest(levels, xs, pend, panels, diag, wanted):
    n = len(levels)
    count = n * (LEVELS - 1 - levels[-1]) + len(wanted)
    out = call(
        functools.partial(forward_rest, levels, wanted),
        (sds((LEVELS, V, 128)), *[sds((V, 128))] * n, *[sds(PARTS, BF16)] * len(wanted)),
        [VM] * n + [VM, HBM, HBM],
        (VM,) * (1 + n + len(wanted)),
        scratch=buffers(count),
        flops=count << 24,
        nbytes=count << 19,
    )(*xs, pend, panels, diag)
    return out[0], out[1 : 1 + n], out[1 + n :]


def forward_last(got_ref, y0, y1, y2, y3, x4_ref, w4_ref, w5_ref, msg_ref):
    y4 = times_columns(x4_ref[...], w4_ref[...])
    y5 = times_columns(columns_of(got_ref, 4), w5_ref[...])
    for k, one in enumerate((y0, y1, y2, y3)):
        msg_ref[pl.ds(16 * k, 16), :] = one[...]
    msg_ref[pl.ds(64, 16), :] = y4
    msg_ref[pl.ds(80, 16), :] = y5


def run_forward_last(got, ys, x4, w4, w5):
    return call(
        forward_last,
        sds((96, 128)),
        [VM] * 8,
        VM,
        flops=2 << 24,
        nbytes=1 << 20,
    )(got, *ys, x4, w4, w5)


def column_message(msg_ref, columns, copies=4):
    for t in range(8):
        turned = block_swap(columns[:, 128 * t : 128 * t + 128])
        for l in range(copies):
            msg_ref[pl.ds(128 * l + 16 * t, 16), :] = turned


def backward_start(own_ref, g1, g2, g3, w_ref, y_ref, msg_ref):
    y = (own_ref[...] + g1[...]) + (g2[...] + g3[...])
    y_ref[...] = y
    column_message(msg_ref, times_rows(y[80:96], w_ref[...]))


def run_backward_start(own, others, w):
    return call(
        backward_start,
        (sds((96, 128)), sds((512, 128))),
        [VM] * 5,
        (VM, VM),
        flops=1 << 24,
        nbytes=1 << 20,
    )(own, *others, w)


def rows_of(got_ref):
    parts = []
    for q in range(4):
        total = got_ref[pl.ds(128 * q, 8), :]
        for t in range(1, 16):
            total += got_ref[pl.ds(128 * q + 8 * t, 8), :]
        parts.append(total[0:4] + total[4:8])
    return block_swap(jnp.concatenate(parts, 0))


def backward_step(level, count, *refs):
    got_ref, pend_ref = refs[:2]
    earlier, blocks, (x_ref, msg_ref) = refs[2 : 1 + count], refs[1 + count : 1 + 2 * count], refs[-2:]
    x = rows_of(got_ref)
    x_ref[...] = x
    columns = pend_ref[level]
    for one, w_ref in zip([r[...] for r in earlier] + [x], blocks):
        columns -= times_rows(one, w_ref[...])
    column_message(msg_ref, columns, 4 if level else 1)


def run_backward_step(level, got, pend, earlier, blocks):
    return call(
        functools.partial(backward_step, level, len(blocks)),
        (sds((V, 128)), sds((512 if level else 128, 128))),
        [VM] * (2 + len(earlier) + len(blocks)),
        (VM, VM),
        flops=len(blocks) << 24,
        nbytes=len(blocks) << 20,
    )(got, pend, *earlier, *blocks)


def backward_next(got_ref, y_ref, diag_ref, w_ref, x_ref, msg_ref):
    x = rows_of(got_ref)
    x_ref[...] = x
    column_message(msg_ref, times_rows(y_ref[64:80, :], diag_ref[...]) - times_rows(x, w_ref[...]))


def run_backward_next(got, y, diag, w):
    return call(
        backward_next,
        (sds((V, 128)), sds((512, 128))),
        [VM] * 4,
        (VM, VM),
        flops=2 << 24,
        nbytes=1 << 20,
    )(got, y, diag, w)


def backward_diag(wanted, y_ref, x_ref, panels_ref, diag_ref, out_ref, *refs):
    w_refs, (buffer, sems) = refs[:-2], refs[-2:]
    pairs = [(up, k) for k in range(LEVELS - 2) for up in (k, LEVELS - 1)] + list(wanted)
    copies = fetch([block_of(panels_ref, diag_ref, *pair) for pair in pairs], buffer, sems)
    for k in range(LEVELS - 2):
        copies[2 * k].wait()
        columns = times_rows(y_ref[pl.ds(16 * k, 16), :], block_parts(buffer[2 * k]))
        copies[2 * k + 1].wait()
        out_ref[k] = columns - times_rows(x_ref[...], block_parts(buffer[2 * k + 1]))
    for n, w_ref in enumerate(w_refs):
        slot = 2 * (LEVELS - 2) + n
        copies[slot].wait()
        w_ref[...] = block_parts(buffer[slot])


def run_backward_diag(y, x, panels, diag, wanted):
    out = call(
        functools.partial(backward_diag, wanted),
        (sds((LEVELS - 2, V, COLS)), *[sds(PARTS, BF16)] * len(wanted)),
        [VM, VM, HBM, HBM],
        (VM,) * (1 + len(wanted)),
        scratch=buffers(2 * (LEVELS - 2) + len(wanted)),
        flops=11 << 24,
        nbytes=6 << 20,
    )(y, x, panels, diag)
    return out[0], out[1:]


def backward_rest(levels, wanted, *refs):
    n = len(levels)
    x_refs, (pend_ref, panels_ref), refs = refs[:n], refs[n : n + 2], refs[n + 2 :]
    out_ref, w_refs, (buffer, sems) = refs[0], refs[1:-2], refs[-2:]
    lower = range(levels[-1] - 2, -1, -1)
    pairs = [(k, j) for j in lower for k in levels] + list(wanted)
    copies = fetch([block_of(panels_ref, None, *pair) for pair in pairs], buffer, sems)
    slot = 0
    for j in lower:
        columns = pend_ref[j]
        for x_ref in x_refs:
            copies[slot].wait()
            columns -= times_rows(x_ref[...], block_parts(buffer[slot]))
            slot += 1
        out_ref[j] = columns
    for w_ref in w_refs:
        copies[slot].wait()
        w_ref[...] = block_parts(buffer[slot])
        slot += 1


def run_backward_rest(levels, xs, pend, panels, wanted):
    n, lower = len(levels), levels[-1] - 1
    count = n * lower + len(wanted)
    out = call(
        functools.partial(backward_rest, levels, wanted),
        (sds((lower, V, COLS)), *[sds(PARTS, BF16)] * len(wanted)),
        [VM] * n + [VM, HBM],
        (VM,) * (1 + len(wanted)),
        scratch=buffers(count),
        flops=count << 24,
        nbytes=count << 19,
    )(*xs, pend, panels)
    return out[0], out[1:]


def own_finish(place_ref, got_ref, x1, x2, x3, x4, x5, index_ref, chunk_ref, msg_ref):
    total = got_ref[pl.ds(0, 8), :]
    for t in range(1, 16):
        total += got_ref[pl.ds(8 * t, 8), :]
    chunk = total[0:4] + total[4:8]
    chunk_ref[...] = jnp.concatenate([chunk] * 2, 0)
    mine = [block_swap(jnp.concatenate([chunk] * 4, 0))[:, :32]]
    for x in [r[...] for r in (x1, x2, x3, x4, x5)]:
        one = jnp.zeros((V, 32), F32)
        for q in range(4):
            one = jnp.where(place_ref[0] == q, x[:, 32 * q : 32 * q + 32], one)
        mine.append(one)
    rows = jnp.concatenate(mine + [jnp.zeros((V, 64), F32)], 1)
    high, low = split(jnp.concatenate([rows] * 8, 0))
    table = jnp.concatenate([high, low], 0).astype(F32)
    index = index_ref[...]
    column = (iota((128, 256), 1) + 1).astype(F32)
    group = (iota((256, 256), 0) >> 4) & 7
    hot, tables = [], []
    for g in range(8):
        pair = [jnp.where(index[:, j : j + 1] == column, 1.0, 0.0) for j in (g, 8 + g)]
        hot.append(jnp.concatenate(pair, 0).astype(BF16))
        tables.append(jnp.where(group == g, table, 0.0).astype(BF16))
    got = dot(jnp.concatenate(hot, 1), jnp.concatenate(tables, 1), NT)
    for half in range(2):
        part = got[128 * half : 128 * half + 128]
        msg_ref[pl.ds(half, 128, 2), :] = part[:, :128] + part[:, 128:]


def run_own_finish(place, got, xs, index):
    return call(
        own_finish,
        (sds((8, 128)), sds((256, 128))),
        [SMEM, VM] + [VM] * 5 + [VM],
        (VM, VM),
        flops=1 << 27,
        nbytes=1 << 20,
    )(place, got, *xs, index)


def write_rows(place_ref, c0, c1, c2, c3, x1, x2, x3, x4, x5, out_ref):
    chunks = [r[0:4, :] for r in (c0, c1, c2, c3)]
    parts = []
    for q in range(4):
        one = jnp.zeros((4, 128), F32)
        for d in range(4):
            one = jnp.where(((place_ref[0] + d) & 3) == q, chunks[d], one)
        parts.append(one)
    for k, x in enumerate([block_swap(jnp.concatenate(parts, 0))] + [r[...] for r in (x1, x2, x3, x4, x5)]):
        for q in range(4):
            out_ref[pl.ds(4 * k + q, V, 4 * LEVELS), :] = x[:, 32 * q : 32 * q + 32]


def run_write_rows(place, chunks, xs):
    return call(
        write_rows,
        sds((V * LEVELS * 4, 32)),
        [SMEM] + [VM] * 9,
        VM,
        flops=1 << 20,
        nbytes=1 << 18,
    )(place, *chunks, *xs)


def exchange(message, axis=ALL):
    return lax.all_to_all(message, axis, 0, 0, tiled=True)


def from_other_leaves(array):
    return [lax.ppermute(array, "leaf", [((l + d) % 4, l) for l in range(4)]) for d in range(1, 4)]


def per_device(leaf_rhs, leaf_inv, update_blocks, row_map, live_rows, sep_rhs, inv_diag, panels):
    place = lax.axis_index("leaf").astype(jnp.int32).reshape(1)
    rhs = sep_rhs.reshape(V, LEVELS * 128)
    leaf_y, message, table, rank = run_leaf_forward(live_rows, leaf_rhs, row_map, leaf_inv, update_blocks)
    got = exchange(message)
    first, far, near = run_first_blocks(leaf_y, panels)
    pend, message, index = run_own_start(place, got, rhs, near)
    got = exchange(message, "sep")
    x0, message = run_forward_step(1, 1, got, pend, [], [first])
    x1, message = run_forward_step(2, 4, exchange(message), pend, [x0], [far, near])
    got = exchange(message)
    pend, (y0, y1), (first, far, near) = run_forward_rest(
        (0, 1), [x0, x1], pend, panels, inv_diag, ((3, 2), (4, 2), (4, 3))
    )
    x2, message = run_forward_step(3, 4, got, pend, [], [first])
    x3, message = run_forward_step(4, 4, exchange(message), pend, [x2], [far, near])
    got = exchange(message)
    pend, (y2, y3), (first, d4, d5) = run_forward_rest(
        (2, 3), [x2, x3], pend, panels, inv_diag, ((5, 4), (4, 4), (5, 5))
    )
    x4, message = run_forward_step(5, 4, got, pend, [], [first])
    message = run_forward_last(exchange(message), [y0, y1, y2, y3], x4, d4, d5)
    y, message = run_backward_start(message, from_other_leaves(message), d5)
    s5, message = run_backward_next(exchange(message), y, d4, first)
    got = exchange(message)
    pend, (first, far, near) = run_backward_diag(y, s5, panels, inv_diag, ((4, 3), (4, 2), (3, 2)))
    s4, message = run_backward_step(3, got, pend, [], [first])
    s3, message = run_backward_step(2, exchange(message), pend, [s4], [far, near])
    got = exchange(message)
    pend, (first, far, near) = run_backward_rest((4, 3), [s4, s3], pend, panels, ((2, 1), (2, 0), (1, 0)))
    s2, message = run_backward_step(1, got, pend, [], [first])
    s1, message = run_backward_step(0, exchange(message), pend, [s2], [far, near])
    xs = [s1, s2, s3, s4, s5]
    chunk, message = run_own_finish(place, exchange(message, "sep"), xs, index)
    got = exchange(message)
    chunks = [chunk, *from_other_leaves(chunk)]
    rows = run_write_rows(place, chunks, xs)
    leaf_x = run_leaf_backward(live_rows, got, table, rank, leaf_y, leaf_inv, update_blocks)
    sep_solution = rows.reshape(V, LEVELS, 4, 1, 32)
    return leaf_x, sep_solution


def solution(mesh):
    in_specs = (
        P(ALL, None, None),
        P(ALL, None, None),
        P(ALL, None, None),
        P(ALL, None),
        P(ALL),
        P(None, None, None, "sep", None),
        P(None, None, "sep", None, "leaf"),
        P(None, None, "sep", None, "leaf"),
    )
    out_specs = (P(ALL, None, None), P(None, None, None, "sep", None))
    return jax.shard_map(per_device, mesh=mesh, in_specs=in_specs, out_specs=out_specs, check_vma=False)
```
